32 devices in a mesh: pair: 2 (over core), grp: 4 (over z), sp: 4 (over y, x).
Axes of the slice: x: 2, y: 2, z: 4, core: 2. Of those that a mesh axis runs over, the one named last changes fastest.
Arguments:
- tokens: bfloat16 [2, 1024, 64, 128], P('pair', ('grp', 'sp')), may hold values from -6 to 6
- owner_ids: int32 [2, 1024, 2], P('pair', ('grp', 'sp')), may hold values from 0 to 15, all different within a row; in each aligned block of 64 rows (0 to 63, 64 to 127, ..., all dimensions but the last counted through in order) at most 16 rows name the same one
- local_ids: int32 [2, 1024, 2], P('pair', ('grp', 'sp')), may hold values from 0 to 63
- weight_qkv: bfloat16 [128, 384], replicated, may hold values from -64 to 64
- weight_out: bfloat16 [128, 128], replicated, may hold values from -0.5 to 0.5
- weight_up: bfloat16 [128, 512], replicated, may hold values from -0.5 to 0.5
- weight_down: bfloat16 [512, 128], replicated, may hold values from -0.25 to 0.25
- cotangent: bfloat16 [2, 1024, 64, 128], P('pair', ('grp', 'sp')), may hold values from -6 to 6
Outputs:
- block_out: bfloat16 [2, 1024, 64, 128], P('pair', ('grp', 'sp'))
- grad_tokens: bfloat16 [2, 1024, 64, 128], P('pair', ('grp', 'sp'))
- grad_qkv: float32 [128, 384], replicated
- grad_out: float32 [128, 128], replicated
- grad_up: float32 [128, 512], replicated
- grad_down: float32 [512, 128], replicated
The draws below stay inside these ranges and needn't reach their ends.
Inputs may be any that keep to these rules, and one draw needn't show every extreme that they name: `owner_ids`: each window names 2 different devices; among the 64 windows of one device no device is named more than 16 times, and some device exactly 16 times.
All inputs are finite; a program needn't handle non-finite values.
Results may differ from the reference program's by a relative error of at most 0.006.
The reference program's roundings to bfloat16 on the way count: a program that leaves them out, or rounds other values in their place, can miss the bound.
Values may be sent and summed in bfloat16 or wider, within the bound.
A program may use at most 128 MiB of HBM per device.

```python
import math
import jax
import jax.numpy as jnp
import numpy as np
from jax import lax

C = 128
HEADS = 4
F = 512
W = 64
K = 2
BD = 64
GROUP = 16
NB = 1024
CAP = 16


def draw_weight_qkv(key, part):
    base = jnp.clip(jax.random.normal(key, (C, 3 * C), jnp.float32), -6.0, 6.0) / math.sqrt(C)
    return base.astype(jnp.bfloat16)


def place_ends(result, own_key, least, top_value):
    longest = result.shape.index(max(result.shape))
    spots = []
    for shift in (0, 1):
        where = [jax.random.randint(jax.random.fold_in(own_key, axis), (), 0, length) for axis, length in enumerate(result.shape)]
        where[longest] = (where[longest] + shift) % result.shape[longest]
        spots.append(tuple(where))
    return result.at[spots[0]].set(least).at[spots[1]].set(top_value)


def shard_levels(rng, extent, pieces, smallest, largest):
    def one(dim, shards_of):
        draws = jax.random.uniform(jax.random.fold_in(jax.random.fold_in(rng, 6), dim), (shards_of,), jnp.float32, smallest / len(pieces), largest / len(pieces))
        return jnp.repeat(jnp.exp(draws), extent[dim] // shards_of).reshape((-1,) + (1,) * (len(extent) - dim - 1))

    level = one(*pieces[0])
    for cut in pieces[1:]:
        level = level * one(*cut)
    return level


def assign_block(rng, own, number, rows, count, top, bound, skew):
    order = jax.random.permutation(rng, count)
    packed, common = shares(count, rows * top, bound, skew, True), shares(count, rows * top, bound, skew, False)
    places = jnp.arange(count)

    def named(tallies, turn):
        used = int((tallies > 0).sum())
        fixed = max(1, used // 4)
        passed = fixed + (places - fixed + turn * (used - fixed)) % max(1, count - fixed)
        return jnp.zeros((count,), jnp.int32).at[order[jnp.where(places < fixed, places, passed)]].set(jnp.asarray(tallies, jnp.int32))

    tallies = jnp.where(number % 4 == 0, named(packed, number // 4), named(common, number - number // 4 - 1))
    mixed = jax.random.permutation(jax.random.fold_in(own, 3), count)
    donor, taker = mixed[0:count // 2 * 2:2], mixed[1:count // 2 * 2:2]
    margin = jnp.minimum(tallies[donor] - 1, bound - tallies[taker]) // 2
    margin = jnp.where((donor == order[0]) | (taker == order[0]) | (tallies[taker] == 0), 0, jnp.maximum(margin, 0))
    passed = jax.random.randint(jax.random.fold_in(own, 4), (count // 2,), 0, 1 << 20) % (margin + 1)
    tallies = tallies.at[donor].add(-passed).at[taker].add(passed)
    members = jnp.searchsorted(jnp.cumsum(tallies), jnp.arange(rows * top), side="right").astype(jnp.int32)
    table = members.reshape(top, rows).T
    table = table[jax.random.permutation(jax.random.fold_in(own, 1), rows)]
    turn = jax.random.randint(jax.random.fold_in(own, 2), (rows, 1), 0, top)
    return jnp.take_along_axis(table, (jnp.arange(top)[None, :] + turn) % top, axis=1)


def shares(count, total, most, skew, full):
    weights = [(1 << 20) // math.isqrt(rank ** skew) + 1 for rank in range(1, count + 1)]
    largest = most if full else min(most, max(-(-total // count), total * weights[0] // sum(weights)))
    least = 1 if total - largest >= count - 1 else 0
    counts, spare = [largest] + [least] * (count - 1), total - largest - least * (count - 1)
    while spare > 0:
        free = [i for i in range(1, count) if counts[i] < largest] or [i for i in range(1, count) if counts[i] < most]
        pool, budget = sum([weights[i] for i in free]), spare
        for i in free:
            addition = min(most - counts[i], max(1, budget * weights[i] // pool), spare)
            counts[i] = counts[i] + addition
            spare = spare - addition
    return np.array(counts)


def normal_values(rng, shape, deviation, most, split=(), kind=jnp.bfloat16):
    array = jax.random.normal(rng, shape, jnp.float32) * deviation
    if len(split) > 0:
        array = shard_levels(rng, shape, split, -0.22, 0.18) * array
    return jnp.clip(array, min=-most, max=most).astype(kind)


def setup_inputs(seed: int = 0) -> dict:
    seeds = jax.random.split(jax.random.key(seed), 9)
    tokens = normal_values(seeds[0], (2, NB, W, C), 1.0, 6.0, ((0, 2), (1, 16)))
    owner_ids_keys = jax.random.split(jax.random.fold_in(seeds[1], 1), 2 * NB // BD)
    owner_ids_turns = jax.random.permutation(jax.random.fold_in(seeds[1], 3), 2 * NB // BD)
    owner_ids = jax.vmap(lambda own, number: assign_block(jax.random.fold_in(seeds[1], 2), own, number, BD, GROUP, K, CAP, 2))(owner_ids_keys, owner_ids_turns).reshape((2, NB, K))
    local_ids = place_ends(jax.random.randint(seeds[2], (2, NB, K), 0, BD), jax.random.fold_in(seeds[2], 1), 0, BD - 1).astype(jnp.int32)
    weight_qkv = draw_weight_qkv(jax.random.fold_in(seeds[8], 71), 0)
    weight_out = normal_values(seeds[4], (C, C), C ** -0.5, 0.5)
    weight_up = normal_values(seeds[5], (C, F), C ** -0.5, 0.5)
    weight_down = normal_values(seeds[6], (F, C), F ** -0.5, 0.25)
    cotangent = normal_values(seeds[7], (2, NB, W, C), 1.0, 6.0, ((0, 2), (1, 16)))
    return dict(tokens=tokens, owner_ids=owner_ids, local_ids=local_ids, weight_qkv=weight_qkv, weight_out=weight_out, weight_up=weight_up, weight_down=weight_down, cotangent=cotangent)


eps_norm = 1e-05
gelu_scale = 0.7978845608028654
gelu_cubic = 0.044715

def norm_rows(values):
    centred = values - lax.optimization_barrier(jnp.mean(values, axis=-1, keepdims=True))
    factor = lax.rsqrt(lax.optimization_barrier(jnp.mean(centred * centred, axis=-1, keepdims=True)) + eps_norm)
    return (centred * factor, factor)

def norm_back(upstream, normed, factor):
    return factor * (upstream - lax.optimization_barrier(jnp.mean(upstream, axis=-1, keepdims=True)) - normed * lax.optimization_barrier(jnp.mean(upstream * normed, axis=-1, keepdims=True)))

def gelu_pair(upper):
    tangent = jnp.tanh(gelu_scale * (upper + gelu_cubic * upper * upper * upper))
    value = 0.5 * upper * (1.0 + tangent)
    slope = 0.5 * (1.0 + tangent) + 0.5 * upper * (1.0 - tangent * tangent) * gelu_scale * (1.0 + 3.0 * gelu_cubic * upper * upper)
    return (value, slope)

def matmul(former, latter):
    return jnp.dot(former, latter, preferred_element_type=jnp.float32)

def against(former, latter):
    return lax.dot_general(former, latter, (((1,), (1,)), ((), ())), preferred_element_type=jnp.float32)

def outer_sum(former, latter):
    return lax.dot_general(former, latter, (((0,), (0,)), ((), ())), preferred_element_type=jnp.float32)

def softmax_rows(scores):
    peak = lax.optimization_barrier(jnp.max(scores, axis=-1, keepdims=True))
    powers = jnp.exp(scores - peak)
    return powers / lax.optimization_barrier(jnp.sum(powers, axis=-1, keepdims=True))

def split_heads(values, heads):
    return values.astype(jnp.float32).reshape(values.shape[0], values.shape[1], heads, values.shape[2] // heads)

def attend(query, kv_cat, heads):
    width = query.shape[-1]
    factor = 1.0 / math.sqrt(width // heads)
    head_query = split_heads(query, heads)
    head_keys = split_heads(kv_cat[..., :width], heads)
    head_values = split_heads(kv_cat[..., width:], heads)
    weights = softmax_rows(jnp.einsum('nqhd,nkhd->nhqk', head_query, head_keys) * factor)
    weights_low = lax.optimization_barrier(weights.astype(jnp.bfloat16)).astype(jnp.float32)
    mixed = jnp.einsum('nhqk,nkhd->nqhd', weights_low, head_values)
    return mixed.reshape(query.shape).astype(jnp.bfloat16)

def attend_back(query, kv_cat, grad_mixed, heads, window_len):
    items, span = (kv_cat.shape[0], kv_cat.shape[1])
    width = query.shape[-1]
    factor = 1.0 / math.sqrt(width // heads)
    head_query = split_heads(query, heads)
    head_keys = split_heads(kv_cat[..., :width], heads)
    head_values = split_heads(kv_cat[..., width:], heads)
    head_grad = split_heads(grad_mixed, heads)
    weights = softmax_rows(jnp.einsum('nqhd,nkhd->nhqk', head_query, head_keys) * factor)
    weights_low = lax.optimization_barrier(weights.astype(jnp.bfloat16)).astype(jnp.float32)
    grad_weights = jnp.einsum('nqhd,nkhd->nhqk', head_grad, head_values)
    centred = grad_weights - lax.optimization_barrier(jnp.sum(grad_weights * weights, axis=-1, keepdims=True))
    grad_scores = (weights * centred * factor).astype(jnp.bfloat16)
    scores_up = lax.optimization_barrier(grad_scores).astype(jnp.float32)
    grad_query = jnp.einsum('nhqk,nkhd->nqhd', scores_up, head_keys).reshape(query.shape)
    grad_keys = jnp.einsum('nhqk,nqhd->nkhd', scores_up, head_query).reshape(items, span, width)
    grad_values = jnp.einsum('nhqk,nqhd->nkhd', weights_low, head_grad).reshape(items, span, width)
    grad_kv = jnp.concatenate([grad_keys, grad_values], axis=-1).reshape(items, span // window_len, window_len, 2 * width)
    return (grad_query, grad_kv[:, 0], grad_kv[:, 1:].astype(jnp.bfloat16))

def tail_forward(rows, mixed, weight_out, weight_up, weight_down):
    resid = lax.optimization_barrier((rows.astype(jnp.float32) + matmul(mixed, weight_out)).astype(jnp.bfloat16))
    normed2, factor2 = norm_rows(resid.astype(jnp.float32))
    normed_low = normed2.astype(jnp.bfloat16)
    value, slope = gelu_pair(matmul(normed_low, weight_up))
    act = value.astype(jnp.bfloat16)
    out_rows = (resid.astype(jnp.float32) + matmul(act, weight_down)).astype(jnp.bfloat16)
    return (out_rows, (normed2, factor2, normed_low, slope, act))

def tail_backward(cot_rows, mixed, saved, weight_out, weight_up, weight_down):
    normed2, factor2, normed_low, slope, act = saved
    grad_upper = (against(cot_rows, weight_down) * slope).astype(jnp.bfloat16)
    grad_resid = cot_rows.astype(jnp.float32) + norm_back(against(grad_upper, weight_up), normed2, factor2)
    grad_resid_low = grad_resid.astype(jnp.bfloat16)
    grad_mixed = against(grad_resid_low, weight_out).astype(jnp.bfloat16)
    grads = (outer_sum(mixed, grad_resid_low), outer_sum(normed_low, grad_upper), outer_sum(act, cot_rows))
    return (grad_resid, grad_mixed, grads)

def reference(tokens, owner_ids, local_ids, weight_qkv, weight_out, weight_up, weight_down, cotangent):
    width = tokens.shape[-1]
    blocks = 2 * NB // BD
    keys_len = (K + 1) * W
    token_blocks = tokens.reshape(blocks, BD * W, width)
    cot_blocks = cotangent.reshape(blocks, BD * W, width)
    partner = (owner_ids * BD + local_ids).astype(jnp.int32).reshape(blocks, BD * K)

    def front_block(rows):
        normed, factor = norm_rows(rows.astype(jnp.float32))
        return matmul(normed.astype(jnp.bfloat16), weight_qkv).astype(jnp.bfloat16)
    qkv_blocks = lax.map(front_block, token_blocks)
    kv_flat = qkv_blocks[..., width:].reshape(2 * NB, W, 2 * width)
    block_index = jnp.arange(blocks, dtype=jnp.int32)

    def first_pass(carry, index):
        accum, out_sum, up_sum, down_sum = carry
        rows = token_blocks[index]
        qkv = qkv_blocks[index].reshape(BD, W, 3 * width)
        other = ((1 - index // (NB // BD)) * NB).astype(jnp.int32)
        targets = other + partner[index]
        far_rows = jnp.take(kv_flat, targets, axis=0).reshape(BD, K, W, 2 * width)
        kv_cat = jnp.concatenate([qkv[:, None, :, width:], far_rows], axis=1).reshape(BD, keys_len, 2 * width)
        query = qkv[..., :width]
        mixed = attend(query, kv_cat, HEADS).reshape(BD * W, width)
        out_rows, saved = tail_forward(rows, mixed, weight_out, weight_up, weight_down)
        grad_resid, grad_mixed, grads = tail_backward(cot_blocks[index], mixed, saved, weight_out, weight_up, weight_down)
        grad_query, self_grad, far_grad = attend_back(query, kv_cat, grad_mixed.reshape(BD, W, width), HEADS, W)
        own_rows = index * BD + jnp.arange(BD, dtype=jnp.int32)
        accum = accum.at[own_rows].add(self_grad)
        far_up = lax.optimization_barrier(far_grad).astype(jnp.float32).reshape(BD * K, W, 2 * width)
        accum = accum.at[targets].add(far_up)
        carry = (accum, out_sum + grads[0], up_sum + grads[1], down_sum + grads[2])
        return (carry, (out_rows, grad_resid, grad_query.reshape(BD * W, width)))
    start = (jnp.zeros((2 * NB, W, 2 * width), jnp.float32), jnp.zeros((width, width), jnp.float32), jnp.zeros((width, F), jnp.float32), jnp.zeros((F, width), jnp.float32))
    carry, outputs = lax.scan(first_pass, start, block_index)
    accum, out_sum, up_sum, down_sum = carry
    out_blocks, grad_resids, grad_queries = outputs

    def second_pass(qkv_sum, index):
        rows = token_blocks[index]
        normed, factor = norm_rows(rows.astype(jnp.float32))
        kv_grad = lax.dynamic_slice_in_dim(accum, (index * BD).astype(jnp.int32), BD, 0).reshape(BD * W, 2 * width)
        grad_rows_qkv = jnp.concatenate([grad_queries[index], kv_grad], axis=1).astype(jnp.bfloat16)
        qkv_sum = qkv_sum + outer_sum(normed.astype(jnp.bfloat16), grad_rows_qkv)
        grad_rows = (grad_resids[index] + norm_back(against(grad_rows_qkv, weight_qkv), normed, factor)).astype(jnp.bfloat16)
        return (qkv_sum, grad_rows)
    qkv_sum, grad_blocks = lax.scan(second_pass, jnp.zeros((width, 3 * width), jnp.float32), block_index)
    inv_count = 1.0 / math.sqrt(2 * NB * W)
    block_out = out_blocks.reshape(2, NB, W, width)
    grad_tokens = grad_blocks.reshape(2, NB, W, width)
    return (block_out, grad_tokens, qkv_sum * inv_count, out_sum * inv_count, up_sum * inv_count, down_sum * inv_count)
```

```python
import functools
import math

import jax
import jax.numpy as jnp
from jax import lax
from jax.experimental import pallas as pl
from jax.experimental.pallas import tpu as pltpu
from jax.sharding import PartitionSpec as P

HEADS = 4
GROUP_SIZE = 4
VMEM_LIMIT = 60 * 1024 * 1024


eps_norm = 1e-05
gelu_scale = 0.7978845608028654
gelu_cubic = 0.044715


def norm_rows(values):
    centred = values - jnp.mean(values, axis=-1, keepdims=True)
    factor = lax.rsqrt(jnp.mean(centred * centred, axis=-1, keepdims=True) + eps_norm)
    return (centred * factor, factor)


def norm_back(upstream, normed, factor):
    return factor * (
        upstream
        - jnp.mean(upstream, axis=-1, keepdims=True)
        - normed * jnp.mean(upstream * normed, axis=-1, keepdims=True)
    )


def gelu_pair(upper):
    squared = upper * upper
    tangent = jnp.tanh(gelu_scale * upper * (1.0 + gelu_cubic * squared))
    half = 0.5 * (1.0 + tangent)
    value = upper * half
    slope = half + 0.5 * upper * (1.0 - tangent * tangent) * (
        gelu_scale + (3.0 * gelu_cubic * gelu_scale) * squared
    )
    return (value, slope)


def matmul(former, latter):
    return jnp.dot(former, latter, preferred_element_type=jnp.float32)


def against(former, latter):
    return lax.dot_general(
        former, latter, (((1,), (1,)), ((), ())), preferred_element_type=jnp.float32
    )


def outer_sum(former, latter):
    return lax.dot_general(
        former, latter, (((0,), (0,)), ((), ())), preferred_element_type=jnp.float32
    )


def head_mask(window_len, width):
    row_head = lax.broadcasted_iota(jnp.int32, (HEADS * window_len, width), 0) // window_len
    col_head = lax.broadcasted_iota(jnp.int32, (HEADS * window_len, width), 1) // (width // HEADS)
    return jnp.where(row_head == col_head, 1.0, 0.0).astype(jnp.bfloat16)


def spread_heads(rows, mask):
    return jnp.concatenate([rows] * HEADS, axis=0) * mask


def gather_heads(full, window_len):
    width = full.shape[-1]
    lane = lax.broadcasted_iota(jnp.int32, (window_len, width), 1) // (width // HEADS)
    result = full[:window_len]
    for head in range(1, HEADS):
        result = jnp.where(lane == head, full[head * window_len : (head + 1) * window_len], result)
    return result


def pick_kernel(wanted, tokens, picked, normed):
    windows, window_len, width = tokens.shape

    @pl.loop(0, windows // 4)
    def _(step):
        rows = tokens[pl.ds(step * 4, 4)].astype(jnp.float32)
        normed[pl.ds(step * 4, 4)] = norm_rows(rows)[0].astype(jnp.bfloat16)

    @pl.loop(0, picked.shape[0] // 8)
    def _(step):
        for inner in range(8):
            slot = step * 8 + inner
            window = jnp.clip(wanted[slot], 0, windows - 1)
            picked[slot] = normed[window]


def main_kernel(
    position,
    tokens,
    cotangent,
    answered,
    weight_qkv,
    weight_out,
    weight_up,
    weight_down,
    block_out,
    grad_resid_out,
    grad_query_out,
    self_grad,
    outbound,
    weight_grads,
    weights_buf,
    kv_buf,
    query_buf,
    mixed_buf,
):
    step = pl.program_id(0)
    window_len = answered.shape[1]
    width = tokens.shape[-1]
    group = tokens.shape[0] // window_len
    fanout = kv_buf.shape[1] // window_len - 1
    factor = 1.0 / math.sqrt(width // HEADS)
    mask = head_mask(window_len, width)

    @pl.when(step == 0)
    def _():
        weight_grads[...] = jnp.zeros_like(weight_grads)

    rows = tokens[...].astype(jnp.float32)
    normed1_low = norm_rows(rows)[0].astype(jnp.bfloat16)
    qkv = matmul(normed1_low, weight_qkv[...]).astype(jnp.bfloat16)
    for item in range(group):
        own = slice(item * window_len, (item + 1) * window_len)
        far = jnp.concatenate(
            [answered[position[(step * group + item) * fanout + j]] for j in range(fanout)], axis=0
        )
        far_kv = matmul(far, weight_qkv[:, width:]).astype(jnp.bfloat16)
        kv = jnp.concatenate([qkv[own, width:], far_kv], axis=0)
        kv_buf[item] = kv
        query = spread_heads(qkv[own, :width], mask)
        query_buf[item] = query
        scores = against(kv[:, :width], query)
        peak = jnp.max(scores, axis=0, keepdims=True)
        powers = jnp.exp((scores - peak) * factor)
        weights = powers * (1.0 / jnp.sum(powers, axis=0, keepdims=True))
        weights_buf[item] = weights
        full = outer_sum(weights.astype(jnp.bfloat16), kv[:, width:])
        mixed_buf[own] = gather_heads(full, window_len).astype(jnp.bfloat16)

    mixed = mixed_buf[...]
    cot = cotangent[...]
    resid = (rows + matmul(mixed, weight_out[...])).astype(jnp.bfloat16).astype(jnp.float32)
    normed2, factor2 = norm_rows(resid)
    normed2_low = normed2.astype(jnp.bfloat16)
    value, slope = gelu_pair(matmul(normed2_low, weight_up[...]))
    act = value.astype(jnp.bfloat16)
    block_out[...] = (resid + matmul(act, weight_down[...])).astype(jnp.bfloat16)
    grad_upper = (against(cot, weight_down[...]) * slope).astype(jnp.bfloat16)
    grad_resid = cot.astype(jnp.float32) + norm_back(
        against(grad_upper, weight_up[...]), normed2, factor2
    )
    grad_resid_out[...] = grad_resid
    grad_resid_low = grad_resid.astype(jnp.bfloat16)
    grad_mixed = against(grad_resid_low, weight_out[...]).astype(jnp.bfloat16)
    grad_out = outer_sum(mixed, grad_resid_low)
    grad_up = outer_sum(normed2_low, grad_upper)
    grad_down = outer_sum(act, cot)
    blocks = grad_upper.shape[-1] // width
    weight_grads[:width] += grad_out
    for block in range(blocks):
        weight_grads[(1 + block) * width : (2 + block) * width] += grad_up[
            :, block * width : (block + 1) * width
        ]
    weight_grads[(1 + blocks) * width :] += grad_down

    for item in range(group):
        own = slice(item * window_len, (item + 1) * window_len)
        kv = kv_buf[item]
        query = query_buf[item]
        weights = weights_buf[item]
        head_grad = spread_heads(grad_mixed[own], mask)
        grad_weights = against(kv[:, width:], head_grad)
        inner = jnp.sum(grad_weights * weights, axis=0, keepdims=True)
        grad_scores = (weights * (grad_weights - inner) * factor).astype(jnp.bfloat16)
        full = outer_sum(grad_scores, kv[:, :width])
        grad_query_out[own] = gather_heads(full, window_len).astype(jnp.bfloat16)
        grad_keys = matmul(grad_scores, query)
        grad_values = matmul(weights.astype(jnp.bfloat16), head_grad)
        self_grad[own, :width] = grad_keys[:window_len]
        self_grad[own, width:] = grad_values[:window_len]
        for j in range(fanout):
            slot = position[(step * group + item) * fanout + j]
            source = slice((j + 1) * window_len, (j + 2) * window_len)
            outbound[slot, :, :width] = grad_keys[source].astype(jnp.bfloat16)
            outbound[slot, :, width:] = grad_values[source].astype(jnp.bfloat16)


def last_kernel(
    wanted, returned, self_grad, grad_query, grad_resid, tokens, weight_qkv, grad_tokens, weight_grads, total
):
    step = pl.program_id(0)
    windows, window_len, width = tokens.shape
    slots = returned.shape[0]

    @pl.when(step == 0)
    def _():
        total[...] = self_grad[...]
        weight_grads[...] = jnp.zeros_like(weight_grads)

    for slot in range(slots):
        window = wanted[step * slots + slot]

        @pl.when(window < windows)
        def _():
            total[window] += returned[slot].astype(jnp.float32)

    @pl.when(step == pl.num_programs(0) - 1)
    def _():
        @pl.loop(0, windows // GROUP_SIZE)
        def _(part):
            span = pl.ds(part * GROUP_SIZE, GROUP_SIZE)
            count = GROUP_SIZE * window_len
            normed1, factor1 = norm_rows(tokens[span].reshape(count, width).astype(jnp.float32))
            grads = jnp.concatenate(
                [
                    grad_query[span].reshape(count, width),
                    total[span].reshape(count, 2 * width).astype(jnp.bfloat16),
                ],
                axis=1,
            )
            upstream = against(grads, weight_qkv[...])
            result = grad_resid[span].reshape(count, width) + norm_back(upstream, normed1, factor1)
            grad_tokens[span] = result.astype(jnp.bfloat16).reshape(GROUP_SIZE, window_len, width)
            sums = outer_sum(normed1.astype(jnp.bfloat16), grads)
            for block in range(3):
                weight_grads[block * width : (block + 1) * width] += sums[
                    :, block * width : (block + 1) * width
                ]


def swapped(value):
    return lax.ppermute(value, "pair", [(0, 1), (1, 0)])


def deliver(parcel):
    return lax.all_to_all(parcel, ("grp", "sp"), split_axis=0, concat_axis=0, tiled=True)


ALL = ("pair", "grp", "sp")


def summed(rows):
    devices = lax.axis_size(ALL)
    share = lax.all_to_all(
        rows.reshape(devices, rows.shape[0] // devices, rows.shape[1]),
        ALL,
        split_axis=0,
        concat_axis=0,
        tiled=True,
    )
    copies = jnp.broadcast_to(jnp.sum(share, axis=0)[None], share.shape)
    copies = lax.all_to_all(copies, ALL, split_axis=0, concat_axis=0, tiled=True)
    return copies.reshape(rows.shape)


def whole(shape):
    return pl.BlockSpec(shape, lambda *_: (0,) * len(shape))


def body(tokens, owner_ids, local_ids, weight_qkv, weight_out, weight_up, weight_down, cotangent):
    holders = lax.axis_size("grp") * lax.axis_size("sp")
    width = tokens.shape[-1]
    hidden = weight_up.shape[-1]
    windows = tokens.shape[1]
    window_len = tokens.shape[2]
    fanout = owner_ids.shape[-1]
    slots = max(2, 2 * windows * fanout // holders)
    keys_len = (fanout + 1) * window_len
    rows_total = windows * window_len
    group = GROUP_SIZE
    group_rows = group * window_len
    token_rows = tokens[0].reshape(rows_total, width)
    cot_rows = cotangent[0].reshape(rows_total, width)
    params = pltpu.CompilerParams(vmem_limit_bytes=VMEM_LIMIT)

    owners = owner_ids[0].reshape(-1)
    local_rows = local_ids[0].reshape(-1)
    onehot = (owners[:, None] == jnp.arange(holders, dtype=jnp.int32)[None, :]).astype(jnp.int32)
    ranks = jnp.sum((jnp.cumsum(onehot, axis=0) - 1) * onehot, axis=1)
    position = owners * slots + ranks
    requests = (
        jnp.full((holders * slots,), windows, jnp.int32)
        .at[position]
        .set(local_rows)
        .reshape(holders, slots)
    )
    wanted_flat = deliver(swapped(requests)).reshape(-1)

    picked = pl.pallas_call(
        pick_kernel,
        grid_spec=pltpu.PrefetchScalarGridSpec(
            num_scalar_prefetch=1,
            grid=(1,),
            in_specs=[whole((windows, window_len, width))],
            out_specs=whole((holders * slots, window_len, width)),
            scratch_shapes=[pltpu.VMEM((windows, window_len, width), jnp.bfloat16)],
        ),
        out_shape=jax.ShapeDtypeStruct((holders * slots, window_len, width), jnp.bfloat16),
        compiler_params=params,
        name="pick",
    )(wanted_flat, tokens[0])
    answered = swapped(deliver(picked.reshape(holders, slots, window_len, width)))
    answered = answered.reshape(holders * slots, window_len, width)

    blocks = hidden // width
    row_spec = pl.BlockSpec((group_rows, width), lambda i, *_: (i, 0))
    out_rows, grad_resid, grad_query, self_grad, outbound, tail_grads = pl.pallas_call(
        main_kernel,
        grid_spec=pltpu.PrefetchScalarGridSpec(
            num_scalar_prefetch=1,
            grid=(windows // group,),
            in_specs=[
                row_spec,
                row_spec,
                whole((holders * slots, window_len, width)),
                whole((width, 3 * width)),
                whole((width, width)),
                whole((width, hidden)),
                whole((hidden, width)),
            ],
            out_specs=[
                row_spec,
                row_spec,
                row_spec,
                pl.BlockSpec((group_rows, 2 * width), lambda i, *_: (i, 0)),
                whole((holders * slots, window_len, 2 * width)),
                whole(((1 + 2 * blocks) * width, width)),
            ],
            scratch_shapes=[
                pltpu.VMEM((group, keys_len, HEADS * window_len), jnp.float32),
                pltpu.VMEM((group, keys_len, 2 * width), jnp.bfloat16),
                pltpu.VMEM((group, HEADS * window_len, width), jnp.bfloat16),
                pltpu.VMEM((group_rows, width), jnp.bfloat16),
            ],
        ),
        out_shape=[
            jax.ShapeDtypeStruct((rows_total, width), jnp.bfloat16),
            jax.ShapeDtypeStruct((rows_total, width), jnp.float32),
            jax.ShapeDtypeStruct((rows_total, width), jnp.bfloat16),
            jax.ShapeDtypeStruct((rows_total, 2 * width), jnp.float32),
            jax.ShapeDtypeStruct((holders * slots, window_len, 2 * width), jnp.bfloat16),
            jax.ShapeDtypeStruct(((1 + 2 * blocks) * width, width), jnp.float32),
        ],
        compiler_params=params,
        name="attend_and_tail",
    )(position, token_rows, cot_rows, answered, weight_qkv, weight_out, weight_up, weight_down)

    returned = deliver(swapped(outbound.reshape(holders, slots, window_len, 2 * width)))
    returned = returned.reshape(holders * slots, window_len, 2 * width)

    grad_rows, qkv_grads = pl.pallas_call(
        last_kernel,
        grid_spec=pltpu.PrefetchScalarGridSpec(
            num_scalar_prefetch=1,
            grid=(holders,),
            in_specs=[
                pl.BlockSpec((slots, window_len, 2 * width), lambda i, *_: (i, 0, 0)),
                whole((windows, window_len, 2 * width)),
                whole((windows, window_len, width)),
                whole((windows, window_len, width)),
                whole((windows, window_len, width)),
                whole((width, 3 * width)),
            ],
            out_specs=[
                whole((windows, window_len, width)),
                whole((3 * width, width)),
            ],
            scratch_shapes=[pltpu.VMEM((windows, window_len, 2 * width), jnp.float32)],
        ),
        out_shape=[
            jax.ShapeDtypeStruct((windows, window_len, width), jnp.bfloat16),
            jax.ShapeDtypeStruct((3 * width, width), jnp.float32),
        ],
        compiler_params=params,
        name="collect",
    )(
        wanted_flat,
        returned,
        self_grad.reshape(windows, window_len, 2 * width),
        grad_query.reshape(windows, window_len, width),
        grad_resid.reshape(windows, window_len, width),
        tokens[0],
        weight_qkv,
    )

    inv_count = 1.0 / math.sqrt(2 * windows * holders * window_len)
    totals = summed(jnp.concatenate([qkv_grads, tail_grads], axis=0)) * inv_count
    sums = totals.reshape(4 + 2 * blocks, width, width)

    def wide(first, count):
        return sums[first : first + count].transpose(1, 0, 2).reshape(width, count * width)

    return (
        out_rows.reshape(1, windows, window_len, width),
        grad_rows[None],
        wide(0, 3),
        sums[3],
        wide(4, blocks),
        sums[4 + blocks :].reshape(hidden, width),
    )


def solution(mesh):
    in_specs = (
        P("pair", ("grp", "sp"), None, None),
        P("pair", ("grp", "sp"), None),
        P("pair", ("grp", "sp"), None),
        P(),
        P(),
        P(),
        P(),
        P("pair", ("grp", "sp"), None, None),
    )
    out_specs = (
        P("pair", ("grp", "sp"), None, None),
        P("pair", ("grp", "sp"), None, None),
        P(),
        P(),
        P(),
        P(),
    )
    return jax.shard_map(body, mesh=mesh, in_specs=in_specs, out_specs=out_specs, check_vma=False)
```

```python
import functools
import math

import jax
import jax.numpy as jnp
from jax import lax
from jax.experimental import pallas as pl
from jax.experimental.pallas import tpu as pltpu
from jax.sharding import PartitionSpec as P

HEADS = 4
GROUP_SIZE = 4
VMEM_LIMIT = 60 * 1024 * 1024


eps_norm = 1e-05
gelu_scale = 0.7978845608028654
gelu_cubic = 0.044715


def norm_rows(values):
    centred = values - jnp.mean(values, axis=-1, keepdims=True)
    factor = lax.rsqrt(jnp.mean(centred * centred, axis=-1, keepdims=True) + eps_norm)
    return (centred * factor, factor)


def norm_back(upstream, normed, factor):
    return factor * (
        upstream
        - jnp.mean(upstream, axis=-1, keepdims=True)
        - normed * jnp.mean(upstream * normed, axis=-1, keepdims=True)
    )


def gelu_pair(upper):
    squared = upper * upper
    tangent = jnp.tanh(gelu_scale * upper * (1.0 + gelu_cubic * squared))
    half = 0.5 * (1.0 + tangent)
    value = upper * half
    slope = half + 0.5 * upper * (1.0 - tangent * tangent) * (
        gelu_scale + (3.0 * gelu_cubic * gelu_scale) * squared
    )
    return (value, slope)


def matmul(former, latter):
    return jnp.dot(former, latter, preferred_element_type=jnp.float32)


def against(former, latter):
    return lax.dot_general(
        former, latter, (((1,), (1,)), ((), ())), preferred_element_type=jnp.float32
    )


def outer_sum(former, latter):
    return lax.dot_general(
        former, latter, (((0,), (0,)), ((), ())), preferred_element_type=jnp.float32
    )


def head_mask(window_len, width):
    row_head = lax.broadcasted_iota(jnp.int32, (HEADS * window_len, width), 0) // window_len
    col_head = lax.broadcasted_iota(jnp.int32, (HEADS * window_len, width), 1) // (width // HEADS)
    return jnp.where(row_head == col_head, 1.0, 0.0).astype(jnp.bfloat16)


def spread_heads(rows, mask):
    return jnp.concatenate([rows] * HEADS, axis=0) * mask


def gather_heads(full, window_len):
    width = full.shape[-1]
    lane = lax.broadcasted_iota(jnp.int32, (window_len, width), 1) // (width // HEADS)
    result = full[:window_len]
    for head in range(1, HEADS):
        result = jnp.where(lane == head, full[head * window_len : (head + 1) * window_len], result)
    return result


def pick_kernel(wanted, tokens, picked, normed):
    windows, window_len, width = tokens.shape

    @pl.loop(0, windows // 4)
    def _(step):
        rows = tokens[pl.ds(step * 4, 4)].astype(jnp.float32)
        normed[pl.ds(step * 4, 4)] = norm_rows(rows)[0].astype(jnp.bfloat16)

    @pl.loop(0, picked.shape[0] // 8)
    def _(step):
        for inner in range(8):
            slot = step * 8 + inner
            window = jnp.clip(wanted[slot], 0, windows - 1)
            picked[slot] = normed[window]


def first_kernel(
    position,
    tokens,
    cotangent,
    answered,
    weight_qkv,
    weight_out,
    weight_up,
    weight_down,
    resid_out,
    normed2_out,
    act_out,
    grad_upper_out,
    grad_resid_out,
    mixed_out,
    grad_mixed_out,
    query_out,
    kv_out,
    weights_out,
    self_values,
    outbound,
):
    step = pl.program_id(0)
    window_len = answered.shape[1]
    width = tokens.shape[-1]
    group = tokens.shape[0] // window_len
    fanout = kv_out.shape[1] // window_len - 1
    factor = 1.0 / math.sqrt(width // HEADS)
    mask = head_mask(window_len, width)

    rows = tokens[...].astype(jnp.float32)
    normed1_low = norm_rows(rows)[0].astype(jnp.bfloat16)
    qkv = matmul(normed1_low, weight_qkv[...]).astype(jnp.bfloat16)
    query_out[...] = qkv[:, :width]
    for item in range(group):
        own = slice(item * window_len, (item + 1) * window_len)
        far = jnp.concatenate(
            [answered[position[(step * group + item) * fanout + j]] for j in range(fanout)], axis=0
        )
        far_kv = matmul(far, weight_qkv[:, width:]).astype(jnp.bfloat16)
        kv = jnp.concatenate([qkv[own, width:], far_kv], axis=0)
        kv_out[item] = kv
        query = spread_heads(qkv[own, :width], mask)
        scores = against(kv[:, :width], query)
        peak = jnp.max(scores, axis=0, keepdims=True)
        powers = jnp.exp((scores - peak) * factor)
        weights = powers * (1.0 / jnp.sum(powers, axis=0, keepdims=True))
        weights_out[item] = weights
        full = outer_sum(weights.astype(jnp.bfloat16), kv[:, width:])
        mixed_out[own] = gather_heads(full, window_len).astype(jnp.bfloat16)

    mixed = mixed_out[...]
    cot = cotangent[...]
    resid_low = (rows + matmul(mixed, weight_out[...])).astype(jnp.bfloat16)
    resid_out[...] = resid_low
    normed2, factor2 = norm_rows(resid_low.astype(jnp.float32))
    normed2_low = normed2.astype(jnp.bfloat16)
    normed2_out[...] = normed2_low
    value, slope = gelu_pair(matmul(normed2_low, weight_up[...]))
    act_out[...] = value.astype(jnp.bfloat16)
    grad_upper = (against(cot, weight_down[...]) * slope).astype(jnp.bfloat16)
    grad_upper_out[...] = grad_upper
    grad_resid = cot.astype(jnp.float32) + norm_back(
        against(grad_upper, weight_up[...]), normed2, factor2
    )
    grad_resid_out[...] = grad_resid
    grad_mixed = against(grad_resid.astype(jnp.bfloat16), weight_out[...]).astype(jnp.bfloat16)
    grad_mixed_out[...] = grad_mixed

    for item in range(group):
        own = slice(item * window_len, (item + 1) * window_len)
        head_grad = spread_heads(grad_mixed[own], mask)
        grad_values = matmul(weights_out[item].astype(jnp.bfloat16), head_grad)
        self_values[own] = grad_values[:window_len]
        for j in range(fanout):
            slot = position[(step * group + item) * fanout + j]
            source = slice((j + 1) * window_len, (j + 2) * window_len)
            outbound[slot] = grad_values[source].astype(jnp.bfloat16)


def second_kernel(
    position,
    tokens,
    cotangent,
    resid,
    normed2_low,
    act,
    grad_upper,
    grad_resid,
    mixed,
    grad_mixed,
    query_rows,
    kv_rows,
    weights_rows,
    weight_down,
    block_out,
    grad_query_out,
    self_keys,
    outbound,
    weight_grads,
):
    step = pl.program_id(0)
    window_len = outbound.shape[1]
    width = cotangent.shape[-1]
    group = cotangent.shape[0] // window_len
    fanout = kv_rows.shape[1] // window_len - 1
    factor = 1.0 / math.sqrt(width // HEADS)
    mask = head_mask(window_len, width)

    @pl.when(step == 0)
    def _():
        weight_grads[...] = jnp.zeros_like(weight_grads)

    for item in range(group):
        own = slice(item * window_len, (item + 1) * window_len)
        kv = kv_rows[item]
        weights = weights_rows[item]
        query = spread_heads(query_rows[own], mask)
        head_grad = spread_heads(grad_mixed[own], mask)
        grad_weights = against(kv[:, width:], head_grad)
        inner = jnp.sum(grad_weights * weights, axis=0, keepdims=True)
        grad_scores = (weights * (grad_weights - inner) * factor).astype(jnp.bfloat16)
        full = outer_sum(grad_scores, kv[:, :width])
        grad_query_out[own] = gather_heads(full, window_len).astype(jnp.bfloat16)
        grad_keys = matmul(grad_scores, query)
        self_keys[own] = grad_keys[:window_len]
        for j in range(fanout):
            slot = position[(step * group + item) * fanout + j]
            source = slice((j + 1) * window_len, (j + 2) * window_len)
            outbound[slot] = grad_keys[source].astype(jnp.bfloat16)

    cot = cotangent[...]
    block_out[...] = (
        resid[...].astype(jnp.float32) + matmul(act[...], weight_down[...])
    ).astype(jnp.bfloat16)
    grad_up = outer_sum(normed2_low[...], grad_upper[...])
    blocks = grad_upper.shape[-1] // width
    normed1_low = norm_rows(tokens[...].astype(jnp.float32))[0].astype(jnp.bfloat16)
    weight_grads[:width] += outer_sum(normed1_low, grad_query_out[...])
    weight_grads[width : 2 * width] += outer_sum(mixed[...], grad_resid[...].astype(jnp.bfloat16))
    for block in range(blocks):
        weight_grads[(2 + block) * width : (3 + block) * width] += grad_up[
            :, block * width : (block + 1) * width
        ]
    weight_grads[(2 + blocks) * width :] += outer_sum(act[...], cot)


def add_returned(wanted, returned, own, total):
    step = pl.program_id(0)
    windows = total.shape[0]
    slots = returned.shape[0]

    @pl.when(step == 0)
    def _():
        total[...] = own[...]

    for slot in range(slots):
        window = wanted[step * slots + slot]

        @pl.when(window < windows)
        def _():
            total[window] += returned[slot].astype(jnp.float32)


def value_kernel(
    wanted, returned, self_values, grad_query, tokens, weight_qkv, upstream, weight_grads, total
):
    windows, window_len, width = tokens.shape
    count = GROUP_SIZE * window_len
    add_returned(wanted, returned, self_values, total)

    @pl.when(pl.program_id(0) == pl.num_programs(0) - 1)
    def _():
        weight_grads[...] = jnp.zeros_like(weight_grads)

        @pl.loop(0, windows // GROUP_SIZE)
        def _(part):
            span = pl.ds(part * GROUP_SIZE, GROUP_SIZE)
            normed1, _ = norm_rows(tokens[span].reshape(count, width).astype(jnp.float32))
            grads = total[span].reshape(count, width).astype(jnp.bfloat16)
            queries = grad_query[span].reshape(count, width)
            partial = against(queries, weight_qkv[:, :width]) + against(
                grads, weight_qkv[:, 2 * width :]
            )
            upstream[span] = partial.reshape(GROUP_SIZE, window_len, width)
            weight_grads[...] += outer_sum(normed1.astype(jnp.bfloat16), grads)


def key_kernel(
    wanted,
    returned,
    self_keys,
    upstream,
    grad_resid,
    tokens,
    weight_qkv,
    grad_tokens,
    weight_grads,
    total,
):
    windows, window_len, width = tokens.shape
    count = GROUP_SIZE * window_len
    add_returned(wanted, returned, self_keys, total)

    @pl.when(pl.program_id(0) == pl.num_programs(0) - 1)
    def _():
        weight_grads[...] = jnp.zeros_like(weight_grads)

        @pl.loop(0, windows // GROUP_SIZE)
        def _(part):
            span = pl.ds(part * GROUP_SIZE, GROUP_SIZE)
            normed1, factor1 = norm_rows(tokens[span].reshape(count, width).astype(jnp.float32))
            grads = total[span].reshape(count, width).astype(jnp.bfloat16)
            towards = upstream[span].reshape(count, width) + against(
                grads, weight_qkv[:, width : 2 * width]
            )
            result = grad_resid[span].reshape(count, width) + norm_back(towards, normed1, factor1)
            grad_tokens[span] = result.astype(jnp.bfloat16).reshape(GROUP_SIZE, window_len, width)
            weight_grads[...] += outer_sum(normed1.astype(jnp.bfloat16), grads)


def swapped(value):
    return lax.ppermute(value, "pair", [(0, 1), (1, 0)])


def deliver(parcel):
    return lax.all_to_all(parcel, ("grp", "sp"), split_axis=0, concat_axis=0, tiled=True)


ALL = ("pair", "grp", "sp")


def summed(rows):
    devices = lax.axis_size(ALL)
    share = lax.all_to_all(
        rows.reshape(devices, rows.shape[0] // devices, rows.shape[1]),
        ALL,
        split_axis=0,
        concat_axis=0,
        tiled=True,
    )
    copies = jnp.broadcast_to(jnp.sum(share, axis=0)[None], share.shape)
    copies = lax.all_to_all(copies, ALL, split_axis=0, concat_axis=0, tiled=True)
    return copies.reshape(rows.shape)


def whole(shape):
    return pl.BlockSpec(shape, lambda *_: (0,) * len(shape))


def body(tokens, owner_ids, local_ids, weight_qkv, weight_out, weight_up, weight_down, cotangent):
    holders = lax.axis_size("grp") * lax.axis_size("sp")
    width = tokens.shape[-1]
    hidden = weight_up.shape[-1]
    windows = tokens.shape[1]
    window_len = tokens.shape[2]
    fanout = owner_ids.shape[-1]
    slots = max(2, 2 * windows * fanout // holders)
    keys_len = (fanout + 1) * window_len
    rows_total = windows * window_len
    group = GROUP_SIZE
    group_rows = group * window_len
    token_rows = tokens[0].reshape(rows_total, width)
    cot_rows = cotangent[0].reshape(rows_total, width)
    params = pltpu.CompilerParams(vmem_limit_bytes=VMEM_LIMIT)

    owners = owner_ids[0].reshape(-1)
    local_rows = local_ids[0].reshape(-1)
    onehot = (owners[:, None] == jnp.arange(holders, dtype=jnp.int32)[None, :]).astype(jnp.int32)
    ranks = jnp.sum((jnp.cumsum(onehot, axis=0) - 1) * onehot, axis=1)
    position = owners * slots + ranks
    requests = (
        jnp.full((holders * slots,), windows, jnp.int32)
        .at[position]
        .set(local_rows)
        .reshape(holders, slots)
    )
    wanted_flat = deliver(swapped(requests)).reshape(-1)

    picked = pl.pallas_call(
        pick_kernel,
        grid_spec=pltpu.PrefetchScalarGridSpec(
            num_scalar_prefetch=1,
            grid=(1,),
            in_specs=[whole((windows, window_len, width))],
            out_specs=whole((holders * slots, window_len, width)),
            scratch_shapes=[pltpu.VMEM((windows, window_len, width), jnp.bfloat16)],
        ),
        out_shape=jax.ShapeDtypeStruct((holders * slots, window_len, width), jnp.bfloat16),
        compiler_params=params,
        name="pick",
    )(wanted_flat, tokens[0])
    answered = swapped(deliver(picked.reshape(holders, slots, window_len, width)))
    answered = answered.reshape(holders * slots, window_len, width)

    blocks = hidden // width
    span_heads = HEADS * window_len
    slot_shape = (holders * slots, window_len, width)
    window_shape = (windows, window_len, width)
    grad_rows_shape = ((2 + 2 * blocks) * width, width)

    def row_spec(lanes):
        return pl.BlockSpec((group_rows, lanes), lambda i, *_: (i, 0))

    def window_spec(lanes):
        return pl.BlockSpec((group, keys_len, lanes), lambda i, *_: (i, 0, 0))

    def row_shape(lanes, kind=jnp.bfloat16):
        return jax.ShapeDtypeStruct((rows_total, lanes), kind)

    saved_specs = [
        row_spec(width),
        row_spec(width),
        row_spec(hidden),
        row_spec(hidden),
        row_spec(width),
        row_spec(width),
        row_spec(width),
        row_spec(width),
        window_spec(2 * width),
        window_spec(span_heads),
    ]
    *saved, self_values, outbound_values = pl.pallas_call(
        first_kernel,
        grid_spec=pltpu.PrefetchScalarGridSpec(
            num_scalar_prefetch=1,
            grid=(windows // group,),
            in_specs=[
                row_spec(width),
                row_spec(width),
                whole(slot_shape),
                whole((width, 3 * width)),
                whole((width, width)),
                whole((width, hidden)),
                whole((hidden, width)),
            ],
            out_specs=saved_specs + [row_spec(width), whole(slot_shape)],
        ),
        out_shape=[
            row_shape(width),
            row_shape(width),
            row_shape(hidden),
            row_shape(hidden),
            row_shape(width, jnp.float32),
            row_shape(width),
            row_shape(width),
            row_shape(width),
            jax.ShapeDtypeStruct((windows, keys_len, 2 * width), jnp.bfloat16),
            jax.ShapeDtypeStruct((windows, keys_len, span_heads), jnp.float32),
            row_shape(width, jnp.float32),
            jax.ShapeDtypeStruct(slot_shape, jnp.bfloat16),
        ],
        compiler_params=params,
        name="attend_and_tail",
    )(position, token_rows, cot_rows, answered, weight_qkv, weight_out, weight_up, weight_down)
    grad_resid = saved[4]

    def across(outbound):
        return swapped(outbound.reshape(holders, slots, window_len, width))

    outgoing_values, saved = lax.optimization_barrier((across(outbound_values), saved))
    returned_values = deliver(outgoing_values).reshape(slot_shape)

    out_rows, grad_query, self_keys, outbound_keys, tail_grads = pl.pallas_call(
        second_kernel,
        grid_spec=pltpu.PrefetchScalarGridSpec(
            num_scalar_prefetch=1,
            grid=(windows // group,),
            in_specs=[row_spec(width), row_spec(width)] + saved_specs + [whole((hidden, width))],
            out_specs=[
                row_spec(width),
                row_spec(width),
                row_spec(width),
                whole(slot_shape),
                whole(grad_rows_shape),
            ],
        ),
        out_shape=[
            row_shape(width),
            row_shape(width),
            row_shape(width, jnp.float32),
            jax.ShapeDtypeStruct(slot_shape, jnp.bfloat16),
            jax.ShapeDtypeStruct(grad_rows_shape, jnp.float32),
        ],
        compiler_params=params,
        cost_estimate=pl.CostEstimate(
            flops=40 * 10**9, bytes_accessed=150 * 10**6, transcendentals=0
        ),
        name="key_gradients",
    )(position, token_rows, cot_rows, *saved, weight_down)

    outgoing_keys, returned_values, grad_query = lax.optimization_barrier(
        (across(outbound_keys), returned_values, grad_query)
    )
    returned_keys = deliver(outgoing_keys).reshape(slot_shape)

    slot_spec = pl.BlockSpec((slots, window_len, width), lambda i, *_: (i, 0, 0))
    collect_scratch = [pltpu.VMEM(window_shape, jnp.float32)]
    upstream, value_grads = pl.pallas_call(
        value_kernel,
        grid_spec=pltpu.PrefetchScalarGridSpec(
            num_scalar_prefetch=1,
            grid=(holders,),
            in_specs=[slot_spec] + [whole(window_shape)] * 3 + [whole((width, 3 * width))],
            out_specs=[whole(window_shape), whole((width, width))],
            scratch_shapes=collect_scratch,
        ),
        out_shape=[
            jax.ShapeDtypeStruct(window_shape, jnp.float32),
            jax.ShapeDtypeStruct((width, width), jnp.float32),
        ],
        compiler_params=params,
        cost_estimate=pl.CostEstimate(
            flops=10 * 10**9, bytes_accessed=50 * 10**6, transcendentals=0
        ),
        name="collect_values",
    )(
        wanted_flat,
        returned_values,
        self_values.reshape(window_shape),
        grad_query.reshape(window_shape),
        tokens[0],
        weight_qkv,
    )
    inv_count = 1.0 / math.sqrt(2 * windows * holders * window_len)
    tail_sums = (lax.psum(tail_grads, ALL) * inv_count).reshape(2 + 2 * blocks, width, width)

    grad_rows, key_grads = pl.pallas_call(
        key_kernel,
        grid_spec=pltpu.PrefetchScalarGridSpec(
            num_scalar_prefetch=1,
            grid=(holders,),
            in_specs=[slot_spec] + [whole(window_shape)] * 4 + [whole((width, 3 * width))],
            out_specs=[whole(window_shape), whole((width, width))],
            scratch_shapes=collect_scratch,
        ),
        out_shape=[
            jax.ShapeDtypeStruct(window_shape, jnp.bfloat16),
            jax.ShapeDtypeStruct((width, width), jnp.float32),
        ],
        compiler_params=params,
        name="collect_keys",
    )(
        wanted_flat,
        returned_keys,
        self_keys.reshape(window_shape),
        upstream,
        grad_resid.reshape(window_shape),
        tokens[0],
        weight_qkv,
    )
    kv_sums = summed(jnp.concatenate([key_grads, value_grads], axis=0)) * inv_count

    return (
        out_rows.reshape(1, windows, window_len, width),
        grad_rows[None],
        jnp.concatenate([tail_sums[0], kv_sums[:width], kv_sums[width:]], axis=1),
        tail_sums[1],
        tail_sums[2 : 2 + blocks].transpose(1, 0, 2).reshape(width, hidden),
        tail_sums[2 + blocks :].reshape(hidden, width),
    )


def solution(mesh):
    in_specs = (
        P("pair", ("grp", "sp"), None, None),
        P("pair", ("grp", "sp"), None),
        P("pair", ("grp", "sp"), None),
        P(),
        P(),
        P(),
        P(),
        P("pair", ("grp", "sp"), None, None),
    )
    out_specs = (
        P("pair", ("grp", "sp"), None, None),
        P("pair", ("grp", "sp"), None, None),
        P(),
        P(),
        P(),
        P(),
    )
    return jax.shard_map(body, mesh=mesh, in_specs=in_specs, out_specs=out_specs, check_vma=False)
```

```python
import functools
import math

import jax
import jax.numpy as jnp
from jax import lax
from jax.experimental import pallas as pl
from jax.experimental.pallas import tpu as pltpu
from jax.sharding import PartitionSpec as P

HEADS = 4
GROUP_SIZE = 4
VMEM_LIMIT = 60 * 1024 * 1024


eps_norm = 1e-05
gelu_scale = 0.7978845608028654
gelu_cubic = 0.044715


def norm_rows(values):
    centred = values - jnp.mean(values, axis=-1, keepdims=True)
    factor = lax.rsqrt(jnp.mean(centred * centred, axis=-1, keepdims=True) + eps_norm)
    return (centred * factor, factor)


def norm_back(upstream, normed, factor):
    return factor * (
        upstream
        - jnp.mean(upstream, axis=-1, keepdims=True)
        - normed * jnp.mean(upstream * normed, axis=-1, keepdims=True)
    )


def gelu_pair(upper):
    squared = upper * upper
    tangent = jnp.tanh(gelu_scale * upper * (1.0 + gelu_cubic * squared))
    half = 0.5 * (1.0 + tangent)
    value = upper * half
    slope = half + 0.5 * upper * (1.0 - tangent * tangent) * (
        gelu_scale + (3.0 * gelu_cubic * gelu_scale) * squared
    )
    return (value, slope)


def matmul(former, latter):
    return jnp.dot(former, latter, preferred_element_type=jnp.float32)


def against(former, latter):
    return lax.dot_general(
        former, latter, (((1,), (1,)), ((), ())), preferred_element_type=jnp.float32
    )


def outer_sum(former, latter):
    return lax.dot_general(
        former, latter, (((0,), (0,)), ((), ())), preferred_element_type=jnp.float32
    )


def head_mask(window_len, width):
    row_head = lax.broadcasted_iota(jnp.int32, (HEADS * window_len, width), 0) // window_len
    col_head = lax.broadcasted_iota(jnp.int32, (HEADS * window_len, width), 1) // (width // HEADS)
    return jnp.where(row_head == col_head, 1.0, 0.0).astype(jnp.bfloat16)


def spread_heads(rows, mask):
    return jnp.concatenate([rows] * HEADS, axis=0) * mask


def gather_heads(full, window_len):
    width = full.shape[-1]
    lane = lax.broadcasted_iota(jnp.int32, (window_len, width), 1) // (width // HEADS)
    result = full[:window_len]
    for head in range(1, HEADS):
        result = jnp.where(lane == head, full[head * window_len : (head + 1) * window_len], result)
    return result


def pick_kernel(wanted, tokens, picked, normed):
    windows, window_len, width = tokens.shape

    @pl.loop(0, windows // 4)
    def _(step):
        rows = tokens[pl.ds(step * 4, 4)].astype(jnp.float32)
        normed[pl.ds(step * 4, 4)] = norm_rows(rows)[0].astype(jnp.bfloat16)

    @pl.loop(0, picked.shape[0] // 8)
    def _(step):
        for inner in range(8):
            slot = step * 8 + inner
            window = jnp.clip(wanted[slot], 0, windows - 1)
            picked[slot] = normed[window]


def first_kernel(
    position,
    tokens,
    cotangent,
    answered,
    weight_qkv,
    weight_out,
    weight_up,
    weight_down,
    resid_out,
    normed2_out,
    act_out,
    grad_upper_out,
    grad_resid_out,
    mixed_out,
    grad_mixed_out,
    query_out,
    kv_out,
    weights_out,
    self_values,
    outbound,
):
    step = pl.program_id(0)
    window_len = answered.shape[1]
    width = tokens.shape[-1]
    group = tokens.shape[0] // window_len
    fanout = kv_out.shape[1] // window_len - 1
    factor = 1.0 / math.sqrt(width // HEADS)
    mask = head_mask(window_len, width)

    rows = tokens[...].astype(jnp.float32)
    normed1_low = norm_rows(rows)[0].astype(jnp.bfloat16)
    qkv = matmul(normed1_low, weight_qkv[...]).astype(jnp.bfloat16)
    query_out[...] = qkv[:, :width]
    for item in range(group):
        own = slice(item * window_len, (item + 1) * window_len)
        far = jnp.concatenate(
            [answered[position[(step * group + item) * fanout + j]] for j in range(fanout)], axis=0
        )
        far_kv = matmul(far, weight_qkv[:, width:]).astype(jnp.bfloat16)
        kv = jnp.concatenate([qkv[own, width:], far_kv], axis=0)
        kv_out[item] = kv
        query = spread_heads(qkv[own, :width], mask)
        scores = against(kv[:, :width], query)
        peak = jnp.max(scores, axis=0, keepdims=True)
        powers = jnp.exp((scores - peak) * factor)
        weights = powers * (1.0 / jnp.sum(powers, axis=0, keepdims=True))
        weights_out[item] = weights
        full = outer_sum(weights.astype(jnp.bfloat16), kv[:, width:])
        mixed_out[own] = gather_heads(full, window_len).astype(jnp.bfloat16)

    mixed = mixed_out[...]
    cot = cotangent[...]
    resid_low = (rows + matmul(mixed, weight_out[...])).astype(jnp.bfloat16)
    resid_out[...] = resid_low
    normed2, factor2 = norm_rows(resid_low.astype(jnp.float32))
    normed2_low = normed2.astype(jnp.bfloat16)
    normed2_out[...] = normed2_low
    value, slope = gelu_pair(matmul(normed2_low, weight_up[...]))
    act_out[...] = value.astype(jnp.bfloat16)
    grad_upper = (against(cot, weight_down[...]) * slope).astype(jnp.bfloat16)
    grad_upper_out[...] = grad_upper
    grad_resid = cot.astype(jnp.float32) + norm_back(
        against(grad_upper, weight_up[...]), normed2, factor2
    )
    grad_resid_out[...] = grad_resid
    grad_mixed = against(grad_resid.astype(jnp.bfloat16), weight_out[...]).astype(jnp.bfloat16)
    grad_mixed_out[...] = grad_mixed

    for item in range(group):
        own = slice(item * window_len, (item + 1) * window_len)
        head_grad = spread_heads(grad_mixed[own], mask)
        grad_values = matmul(weights_out[item].astype(jnp.bfloat16), head_grad)
        self_values[own] = grad_values[:window_len]
        for j in range(fanout):
            slot = position[(step * group + item) * fanout + j]
            source = slice((j + 1) * window_len, (j + 2) * window_len)
            outbound[slot] = grad_values[source].astype(jnp.bfloat16)


def second_kernel(
    position,
    tokens,
    cotangent,
    resid,
    normed2_low,
    act,
    grad_upper,
    grad_resid,
    mixed,
    grad_mixed,
    query_rows,
    kv_rows,
    weights_rows,
    weight_down,
    block_out,
    grad_query_out,
    self_keys,
    outbound,
    weight_grads,
):
    step = pl.program_id(0)
    window_len = outbound.shape[1]
    width = cotangent.shape[-1]
    group = cotangent.shape[0] // window_len
    fanout = kv_rows.shape[1] // window_len - 1
    factor = 1.0 / math.sqrt(width // HEADS)
    mask = head_mask(window_len, width)

    @pl.when(step == 0)
    def _():
        weight_grads[...] = jnp.zeros_like(weight_grads)

    for item in range(group):
        own = slice(item * window_len, (item + 1) * window_len)
        kv = kv_rows[item]
        weights = weights_rows[item]
        query = spread_heads(query_rows[own], mask)
        head_grad = spread_heads(grad_mixed[own], mask)
        grad_weights = against(kv[:, width:], head_grad)
        inner = jnp.sum(grad_weights * weights, axis=0, keepdims=True)
        grad_scores = (weights * (grad_weights - inner) * factor).astype(jnp.bfloat16)
        full = outer_sum(grad_scores, kv[:, :width])
        grad_query_out[own] = gather_heads(full, window_len).astype(jnp.bfloat16)
        grad_keys = matmul(grad_scores, query)
        self_keys[own] = grad_keys[:window_len]
        for j in range(fanout):
            slot = position[(step * group + item) * fanout + j]
            source = slice((j + 1) * window_len, (j + 2) * window_len)
            outbound[slot] = grad_keys[source].astype(jnp.bfloat16)

    cot = cotangent[...]
    block_out[...] = (
        resid[...].astype(jnp.float32) + matmul(act[...], weight_down[...])
    ).astype(jnp.bfloat16)
    grad_up = outer_sum(normed2_low[...], grad_upper[...])
    blocks = grad_upper.shape[-1] // width
    normed1_low = norm_rows(tokens[...].astype(jnp.float32))[0].astype(jnp.bfloat16)
    weight_grads[:width] += outer_sum(normed1_low, grad_query_out[...])
    weight_grads[width : 2 * width] += outer_sum(mixed[...], grad_resid[...].astype(jnp.bfloat16))
    for block in range(blocks):
        weight_grads[(2 + block) * width : (3 + block) * width] += grad_up[
            :, block * width : (block + 1) * width
        ]
    weight_grads[(2 + blocks) * width :] += outer_sum(act[...], cot)


def add_returned(wanted, returned, own, total):
    step = pl.program_id(0)
    windows = total.shape[0]
    slots = returned.shape[0]

    @pl.when(step == 0)
    def _():
        total[...] = own[...]

    for slot in range(slots):
        window = wanted[step * slots + slot]

        @pl.when(window < windows)
        def _():
            total[window] += returned[slot].astype(jnp.float32)


def value_kernel(
    wanted, returned, self_values, grad_query, tokens, weight_qkv, upstream, weight_grads, total
):
    windows, window_len, width = tokens.shape
    count = GROUP_SIZE * window_len
    add_returned(wanted, returned, self_values, total)

    @pl.when(pl.program_id(0) == pl.num_programs(0) - 1)
    def _():
        weight_grads[...] = jnp.zeros_like(weight_grads)

        @pl.loop(0, windows // GROUP_SIZE)
        def _(part):
            span = pl.ds(part * GROUP_SIZE, GROUP_SIZE)
            normed1, _ = norm_rows(tokens[span].reshape(count, width).astype(jnp.float32))
            grads = total[span].reshape(count, width).astype(jnp.bfloat16)
            queries = grad_query[span].reshape(count, width)
            partial = against(queries, weight_qkv[:, :width]) + against(
                grads, weight_qkv[:, 2 * width :]
            )
            upstream[span] = partial.reshape(GROUP_SIZE, window_len, width)
            weight_grads[...] += outer_sum(normed1.astype(jnp.bfloat16), grads)


def key_kernel(
    wanted,
    returned,
    self_keys,
    upstream,
    grad_resid,
    tokens,
    weight_qkv,
    grad_tokens,
    weight_grads,
    total,
):
    windows, window_len, width = tokens.shape
    count = GROUP_SIZE * window_len
    add_returned(wanted, returned, self_keys, total)

    @pl.when(pl.program_id(0) == pl.num_programs(0) - 1)
    def _():
        weight_grads[...] = jnp.zeros_like(weight_grads)

        @pl.loop(0, windows // GROUP_SIZE)
        def _(part):
            span = pl.ds(part * GROUP_SIZE, GROUP_SIZE)
            normed1, factor1 = norm_rows(tokens[span].reshape(count, width).astype(jnp.float32))
            grads = total[span].reshape(count, width).astype(jnp.bfloat16)
            towards = upstream[span].reshape(count, width) + against(
                grads, weight_qkv[:, width : 2 * width]
            )
            result = grad_resid[span].reshape(count, width) + norm_back(towards, normed1, factor1)
            grad_tokens[span] = result.astype(jnp.bfloat16).reshape(GROUP_SIZE, window_len, width)
            weight_grads[...] += outer_sum(normed1.astype(jnp.bfloat16), grads)


def swapped(value):
    return lax.ppermute(value, "pair", [(0, 1), (1, 0)])


def deliver(parcel):
    return lax.all_to_all(parcel, ("grp", "sp"), split_axis=0, concat_axis=0, tiled=True)


ALL = ("pair", "grp", "sp")


def sum_kernel(scatter, scale, rows, total, pair_part, pair_sum, sp_part, sp_sum, grp_part, mine, sp_full, half, pair_full, send_sems, recv_sems):
    sizes = {axis: lax.axis_size(axis) for axis in ALL}
    place = {axis: lax.axis_index(axis) for axis in ALL}
    used = [0]

    barrier = pltpu.get_barrier_semaphore()
    for axis in ALL:
        for hop in range(1, sizes[axis]):
            pl.semaphore_signal(
                barrier,
                inc=1,
                device_id={axis: lax.rem(place[axis] + hop, sizes[axis])},
                device_id_type=pl.DeviceIdType.MESH,
            )
    pl.semaphore_wait(barrier, sum(sizes[axis] - 1 for axis in ALL))

    def exchange(axis, source, landing):
        copies = []
        for hop in range(1, sizes[axis]):
            target = lax.rem(place[axis] + hop, sizes[axis])
            copy = pltpu.make_async_remote_copy(
                src_ref=source(target),
                dst_ref=landing.at[place[axis]],
                send_sem=send_sems.at[used[0]],
                recv_sem=recv_sems.at[used[0]],
                device_id={axis: target},
                device_id_type=pl.DeviceIdType.MESH,
            )
            copy.start()
            used[0] += 1
            copies.append(copy)
        landing[place[axis]] = source(place[axis])[...]
        for copy in copies:
            copy.wait()

    def added(landing):
        result = landing[0]
        for index in range(1, landing.shape[0]):
            result = result + landing[index]
        return result

    exchange("pair", lambda target: rows.at[target], pair_part)
    pieces, count, _ = pair_sum.shape
    for piece in range(pieces):
        span = slice(piece * count, (piece + 1) * count)
        pair_sum[piece] = pair_part[0, span] + pair_part[1, span]
    exchange("sp", (lambda target: pair_sum.at[target]) if scatter else (lambda _: pair_sum.at[0]), sp_part)
    sp_sum[...] = added(sp_part)
    exchange("grp", lambda _: sp_sum, grp_part)
    mine[...] = added(grp_part) * scale
    if scatter:
        exchange("sp", lambda _: mine, sp_full)
        for piece in range(pieces):
            half[piece * count : (piece + 1) * count] = sp_full[piece]
        exchange("pair", lambda _: half, pair_full)
    else:
        exchange("pair", lambda _: mine, pair_full)
    total[...] = pair_full[...]


def summed(rows, scale, collective_id):
    sp, grp = lax.axis_size("sp"), lax.axis_size("grp")
    half, width = rows.shape[0] // 2, rows.shape[1]
    scatter = half % (8 * sp) == 0
    pieces = sp if scatter else 1
    count = half // pieces
    copies = 2 + 2 * (sp - 1) + (grp - 1)

    def buffer(*shape):
        return pltpu.VMEM(shape + (width,), jnp.float32)

    total = pl.pallas_call(
        functools.partial(sum_kernel, scatter, scale),
        in_specs=[pl.BlockSpec(memory_space=pltpu.VMEM)],
        out_specs=pl.BlockSpec(memory_space=pltpu.VMEM),
        out_shape=jax.ShapeDtypeStruct((2, half, width), jnp.float32),
        scratch_shapes=[
            buffer(2, half),
            buffer(pieces, count),
            buffer(sp, count),
            buffer(count),
            buffer(grp, count),
            buffer(count),
            buffer(sp, count),
            buffer(half),
            buffer(2, half),
            pltpu.SemaphoreType.DMA((copies,)),
            pltpu.SemaphoreType.DMA((copies,)),
        ],
        compiler_params=pltpu.CompilerParams(
            collective_id=collective_id, has_side_effects=True, vmem_limit_bytes=32 * 1024 * 1024
        ),
        name="sum_gradients_%d" % collective_id,
    )(rows.reshape(2, half, width))
    return total.reshape(rows.shape)


def whole(shape):
    return pl.BlockSpec(shape, lambda *_: (0,) * len(shape))


def body(tokens, owner_ids, local_ids, weight_qkv, weight_out, weight_up, weight_down, cotangent):
    holders = lax.axis_size("grp") * lax.axis_size("sp")
    width = tokens.shape[-1]
    hidden = weight_up.shape[-1]
    windows = tokens.shape[1]
    window_len = tokens.shape[2]
    fanout = owner_ids.shape[-1]
    slots = max(2, 2 * windows * fanout // holders)
    keys_len = (fanout + 1) * window_len
    rows_total = windows * window_len
    group = GROUP_SIZE
    group_rows = group * window_len
    token_rows = tokens[0].reshape(rows_total, width)
    cot_rows = cotangent[0].reshape(rows_total, width)
    params = pltpu.CompilerParams(vmem_limit_bytes=VMEM_LIMIT)

    owners = owner_ids[0].reshape(-1)
    local_rows = local_ids[0].reshape(-1)
    onehot = (owners[:, None] == jnp.arange(holders, dtype=jnp.int32)[None, :]).astype(jnp.int32)
    ranks = jnp.sum((jnp.cumsum(onehot, axis=0) - 1) * onehot, axis=1)
    position = owners * slots + ranks
    requests = (
        jnp.full((holders * slots,), windows, jnp.int32)
        .at[position]
        .set(local_rows)
        .reshape(holders, slots)
    )
    wanted_flat = deliver(swapped(requests)).reshape(-1)

    picked = pl.pallas_call(
        pick_kernel,
        grid_spec=pltpu.PrefetchScalarGridSpec(
            num_scalar_prefetch=1,
            grid=(1,),
            in_specs=[whole((windows, window_len, width))],
            out_specs=whole((holders * slots, window_len, width)),
            scratch_shapes=[pltpu.VMEM((windows, window_len, width), jnp.bfloat16)],
        ),
        out_shape=jax.ShapeDtypeStruct((holders * slots, window_len, width), jnp.bfloat16),
        compiler_params=params,
        name="pick",
    )(wanted_flat, tokens[0])
    answered = swapped(deliver(picked.reshape(holders, slots, window_len, width)))
    answered = answered.reshape(holders * slots, window_len, width)

    blocks = hidden // width
    span_heads = HEADS * window_len
    slot_shape = (holders * slots, window_len, width)
    window_shape = (windows, window_len, width)
    grad_rows_shape = ((2 + 2 * blocks) * width, width)

    def row_spec(lanes):
        return pl.BlockSpec((group_rows, lanes), lambda i, *_: (i, 0))

    def window_spec(lanes):
        return pl.BlockSpec((group, keys_len, lanes), lambda i, *_: (i, 0, 0))

    def row_shape(lanes, kind=jnp.bfloat16):
        return jax.ShapeDtypeStruct((rows_total, lanes), kind)

    saved_specs = [
        row_spec(width),
        row_spec(width),
        row_spec(hidden),
        row_spec(hidden),
        row_spec(width),
        row_spec(width),
        row_spec(width),
        row_spec(width),
        window_spec(2 * width),
        window_spec(span_heads),
    ]
    *saved, self_values, outbound_values = pl.pallas_call(
        first_kernel,
        grid_spec=pltpu.PrefetchScalarGridSpec(
            num_scalar_prefetch=1,
            grid=(windows // group,),
            in_specs=[
                row_spec(width),
                row_spec(width),
                whole(slot_shape),
                whole((width, 3 * width)),
                whole((width, width)),
                whole((width, hidden)),
                whole((hidden, width)),
            ],
            out_specs=saved_specs + [row_spec(width), whole(slot_shape)],
        ),
        out_shape=[
            row_shape(width),
            row_shape(width),
            row_shape(hidden),
            row_shape(hidden),
            row_shape(width, jnp.float32),
            row_shape(width),
            row_shape(width),
            row_shape(width),
            jax.ShapeDtypeStruct((windows, keys_len, 2 * width), jnp.bfloat16),
            jax.ShapeDtypeStruct((windows, keys_len, span_heads), jnp.float32),
            row_shape(width, jnp.float32),
            jax.ShapeDtypeStruct(slot_shape, jnp.bfloat16),
        ],
        compiler_params=params,
        name="attend_and_tail",
    )(position, token_rows, cot_rows, answered, weight_qkv, weight_out, weight_up, weight_down)
    grad_resid = saved[4]

    def across(outbound):
        return swapped(outbound.reshape(holders, slots, window_len, width))

    outgoing_values, saved = lax.optimization_barrier((across(outbound_values), saved))
    returned_values = deliver(outgoing_values).reshape(slot_shape)

    out_rows, grad_query, self_keys, outbound_keys, tail_grads = pl.pallas_call(
        second_kernel,
        grid_spec=pltpu.PrefetchScalarGridSpec(
            num_scalar_prefetch=1,
            grid=(windows // group,),
            in_specs=[row_spec(width), row_spec(width)] + saved_specs + [whole((hidden, width))],
            out_specs=[
                row_spec(width),
                row_spec(width),
                row_spec(width),
                whole(slot_shape),
                whole(grad_rows_shape),
            ],
        ),
        out_shape=[
            row_shape(width),
            row_shape(width),
            row_shape(width, jnp.float32),
            jax.ShapeDtypeStruct(slot_shape, jnp.bfloat16),
            jax.ShapeDtypeStruct(grad_rows_shape, jnp.float32),
        ],
        compiler_params=params,
        cost_estimate=pl.CostEstimate(
            flops=40 * 10**9, bytes_accessed=150 * 10**6, transcendentals=0
        ),
        name="key_gradients",
    )(position, token_rows, cot_rows, *saved, weight_down)

    outgoing_keys, returned_values, grad_query = lax.optimization_barrier(
        (across(outbound_keys), returned_values, grad_query)
    )
    returned_keys = deliver(outgoing_keys).reshape(slot_shape)

    slot_spec = pl.BlockSpec((slots, window_len, width), lambda i, *_: (i, 0, 0))
    collect_scratch = [pltpu.VMEM(window_shape, jnp.float32)]
    upstream, value_grads = pl.pallas_call(
        value_kernel,
        grid_spec=pltpu.PrefetchScalarGridSpec(
            num_scalar_prefetch=1,
            grid=(holders,),
            in_specs=[slot_spec] + [whole(window_shape)] * 3 + [whole((width, 3 * width))],
            out_specs=[whole(window_shape), whole((width, width))],
            scratch_shapes=collect_scratch,
        ),
        out_shape=[
            jax.ShapeDtypeStruct(window_shape, jnp.float32),
            jax.ShapeDtypeStruct((width, width), jnp.float32),
        ],
        compiler_params=params,
        cost_estimate=pl.CostEstimate(
            flops=10 * 10**9, bytes_accessed=50 * 10**6, transcendentals=0
        ),
        name="collect_values",
    )(
        wanted_flat,
        returned_values,
        self_values.reshape(window_shape),
        grad_query.reshape(window_shape),
        tokens[0],
        weight_qkv,
    )
    inv_count = 1.0 / math.sqrt(2 * windows * holders * window_len)
    early = jnp.concatenate([tail_grads, value_grads, jnp.zeros_like(value_grads)], axis=0)
    tail_sums = summed(early, inv_count, 0).reshape(4 + 2 * blocks, width, width)

    returned_keys, tail_sums = lax.optimization_barrier((returned_keys, tail_sums))
    grad_rows, key_grads = pl.pallas_call(
        key_kernel,
        grid_spec=pltpu.PrefetchScalarGridSpec(
            num_scalar_prefetch=1,
            grid=(holders,),
            in_specs=[slot_spec] + [whole(window_shape)] * 4 + [whole((width, 3 * width))],
            out_specs=[whole(window_shape), whole((width, width))],
            scratch_shapes=collect_scratch,
        ),
        out_shape=[
            jax.ShapeDtypeStruct(window_shape, jnp.bfloat16),
            jax.ShapeDtypeStruct((width, width), jnp.float32),
        ],
        compiler_params=params,
        name="collect_keys",
    )(
        wanted_flat,
        returned_keys,
        self_keys.reshape(window_shape),
        upstream,
        grad_resid.reshape(window_shape),
        tokens[0],
        weight_qkv,
    )
    key_sums = summed(key_grads, inv_count, 1)

    return (
        out_rows.reshape(1, windows, window_len, width),
        grad_rows[None],
        jnp.concatenate([tail_sums[0], key_sums, tail_sums[2 + 2 * blocks]], axis=1),
        tail_sums[1],
        tail_sums[2 : 2 + blocks].transpose(1, 0, 2).reshape(width, hidden),
        tail_sums[2 + blocks : 2 + 2 * blocks].reshape(hidden, width),
    )


def solution(mesh):
    in_specs = (
        P("pair", ("grp", "sp"), None, None),
        P("pair", ("grp", "sp"), None),
        P("pair", ("grp", "sp"), None),
        P(),
        P(),
        P(),
        P(),
        P("pair", ("grp", "sp"), None, None),
    )
    out_specs = (
        P("pair", ("grp", "sp"), None, None),
        P("pair", ("grp", "sp"), None, None),
        P(),
        P(),
        P(),
        P(),
    )
    return jax.shard_map(body, mesh=mesh, in_specs=in_specs, out_specs=out_specs, check_vma=False)
```

```python
import functools
import math

import jax
import jax.numpy as jnp
from jax import lax
from jax.experimental import pallas as pl
from jax.experimental.pallas import tpu as pltpu
from jax.sharding import PartitionSpec as P

HEADS = 4
GROUP_SIZE = 4
VMEM_LIMIT = 60 * 1024 * 1024


eps_norm = 1e-05
gelu_scale = 0.7978845608028654
gelu_cubic = 0.044715


def norm_rows(values):
    centred = values - jnp.mean(values, axis=-1, keepdims=True)
    factor = lax.rsqrt(jnp.mean(centred * centred, axis=-1, keepdims=True) + eps_norm)
    return (centred * factor, factor)


def norm_back(upstream, normed, factor):
    return factor * (
        upstream
        - jnp.mean(upstream, axis=-1, keepdims=True)
        - normed * jnp.mean(upstream * normed, axis=-1, keepdims=True)
    )


def gelu_pair(upper):
    squared = upper * upper
    tangent = jnp.tanh(gelu_scale * upper * (1.0 + gelu_cubic * squared))
    half = 0.5 * (1.0 + tangent)
    value = upper * half
    slope = half + 0.5 * upper * (1.0 - tangent * tangent) * (
        gelu_scale + (3.0 * gelu_cubic * gelu_scale) * squared
    )
    return (value, slope)


def matmul(former, latter):
    return jnp.dot(former, latter, preferred_element_type=jnp.float32)


def against(former, latter):
    return lax.dot_general(
        former, latter, (((1,), (1,)), ((), ())), preferred_element_type=jnp.float32
    )


def outer_sum(former, latter):
    return lax.dot_general(
        former, latter, (((0,), (0,)), ((), ())), preferred_element_type=jnp.float32
    )


def head_mask(window_len, width):
    row_head = lax.broadcasted_iota(jnp.int32, (HEADS * window_len, width), 0) // window_len
    col_head = lax.broadcasted_iota(jnp.int32, (HEADS * window_len, width), 1) // (width // HEADS)
    return jnp.where(row_head == col_head, 1.0, 0.0).astype(jnp.bfloat16)


def spread_heads(rows, mask):
    return jnp.concatenate([rows] * HEADS, axis=0) * mask


def gather_heads(full, window_len):
    width = full.shape[-1]
    lane = lax.broadcasted_iota(jnp.int32, (window_len, width), 1) // (width // HEADS)
    result = full[:window_len]
    for head in range(1, HEADS):
        result = jnp.where(lane == head, full[head * window_len : (head + 1) * window_len], result)
    return result


def pick_kernel(wanted, tokens, picked, normed):
    windows, window_len, width = tokens.shape

    @pl.loop(0, windows // 4)
    def _(step):
        rows = tokens[pl.ds(step * 4, 4)].astype(jnp.float32)
        normed[pl.ds(step * 4, 4)] = norm_rows(rows)[0].astype(jnp.bfloat16)

    @pl.loop(0, picked.shape[0] // 8)
    def _(step):
        for inner in range(8):
            slot = step * 8 + inner
            window = jnp.clip(wanted[slot], 0, windows - 1)
            picked[slot] = normed[window]


def first_kernel(
    position,
    tokens,
    cotangent,
    answered,
    weight_qkv,
    weight_out,
    weight_up,
    weight_down,
    resid_out,
    normed2_out,
    act_out,
    grad_upper_out,
    grad_resid_out,
    mixed_out,
    grad_mixed_out,
    query_out,
    kv_out,
    weights_out,
    self_values,
    outbound,
):
    step = pl.program_id(0)
    window_len = answered.shape[1]
    width = tokens.shape[-1]
    group = tokens.shape[0] // window_len
    fanout = kv_out.shape[1] // window_len - 1
    factor = 1.0 / math.sqrt(width // HEADS)
    mask = head_mask(window_len, width)

    rows = tokens[...].astype(jnp.float32)
    normed1_low = norm_rows(rows)[0].astype(jnp.bfloat16)
    qkv = matmul(normed1_low, weight_qkv[...]).astype(jnp.bfloat16)
    query_out[...] = qkv[:, :width]
    for item in range(group):
        own = slice(item * window_len, (item + 1) * window_len)
        far = jnp.concatenate(
            [answered[position[(step * group + item) * fanout + j]] for j in range(fanout)], axis=0
        )
        far_kv = matmul(far, weight_qkv[:, width:]).astype(jnp.bfloat16)
        kv = jnp.concatenate([qkv[own, width:], far_kv], axis=0)
        kv_out[item] = kv
        query = spread_heads(qkv[own, :width], mask)
        scores = against(kv[:, :width], query)
        peak = jnp.max(scores, axis=0, keepdims=True)
        powers = jnp.exp((scores - peak) * factor)
        weights = powers * (1.0 / jnp.sum(powers, axis=0, keepdims=True))
        weights_out[item] = weights
        full = outer_sum(weights.astype(jnp.bfloat16), kv[:, width:])
        mixed_out[own] = gather_heads(full, window_len).astype(jnp.bfloat16)

    mixed = mixed_out[...]
    cot = cotangent[...]
    resid_low = (rows + matmul(mixed, weight_out[...])).astype(jnp.bfloat16)
    resid_out[...] = resid_low
    normed2, factor2 = norm_rows(resid_low.astype(jnp.float32))
    normed2_low = normed2.astype(jnp.bfloat16)
    normed2_out[...] = normed2_low
    value, slope = gelu_pair(matmul(normed2_low, weight_up[...]))
    act_out[...] = value.astype(jnp.bfloat16)
    grad_upper = (against(cot, weight_down[...]) * slope).astype(jnp.bfloat16)
    grad_upper_out[...] = grad_upper
    grad_resid = cot.astype(jnp.float32) + norm_back(
        against(grad_upper, weight_up[...]), normed2, factor2
    )
    grad_resid_out[...] = grad_resid
    grad_mixed = against(grad_resid.astype(jnp.bfloat16), weight_out[...]).astype(jnp.bfloat16)
    grad_mixed_out[...] = grad_mixed

    for item in range(group):
        own = slice(item * window_len, (item + 1) * window_len)
        head_grad = spread_heads(grad_mixed[own], mask)
        grad_values = matmul(weights_out[item].astype(jnp.bfloat16), head_grad)
        self_values[own] = grad_values[:window_len]
        for j in range(fanout):
            slot = position[(step * group + item) * fanout + j]
            source = slice((j + 1) * window_len, (j + 2) * window_len)
            outbound[slot] = grad_values[source].astype(jnp.bfloat16)


def second_kernel(
    position,
    tokens,
    cotangent,
    resid,
    normed2_low,
    act,
    grad_upper,
    grad_resid,
    mixed,
    grad_mixed,
    query_rows,
    kv_rows,
    weights_rows,
    weight_down,
    block_out,
    grad_query_out,
    self_keys,
    outbound,
    weight_grads,
):
    step = pl.program_id(0)
    window_len = outbound.shape[1]
    width = cotangent.shape[-1]
    group = cotangent.shape[0] // window_len
    fanout = kv_rows.shape[1] // window_len - 1
    factor = 1.0 / math.sqrt(width // HEADS)
    mask = head_mask(window_len, width)

    @pl.when(step == 0)
    def _():
        weight_grads[...] = jnp.zeros_like(weight_grads)

    for item in range(group):
        own = slice(item * window_len, (item + 1) * window_len)
        kv = kv_rows[item]
        weights = weights_rows[item]
        query = spread_heads(query_rows[own], mask)
        head_grad = spread_heads(grad_mixed[own], mask)
        grad_weights = against(kv[:, width:], head_grad)
        inner = jnp.sum(grad_weights * weights, axis=0, keepdims=True)
        grad_scores = (weights * (grad_weights - inner) * factor).astype(jnp.bfloat16)
        full = outer_sum(grad_scores, kv[:, :width])
        grad_query_out[own] = gather_heads(full, window_len).astype(jnp.bfloat16)
        grad_keys = matmul(grad_scores, query)
        self_keys[own] = grad_keys[:window_len]
        for j in range(fanout):
            slot = position[(step * group + item) * fanout + j]
            source = slice((j + 1) * window_len, (j + 2) * window_len)
            outbound[slot] = grad_keys[source].astype(jnp.bfloat16)

    cot = cotangent[...]
    block_out[...] = (
        resid[...].astype(jnp.float32) + matmul(act[...], weight_down[...])
    ).astype(jnp.bfloat16)
    grad_up = outer_sum(normed2_low[...], grad_upper[...])
    blocks = grad_upper.shape[-1] // width
    normed1_low = norm_rows(tokens[...].astype(jnp.float32))[0].astype(jnp.bfloat16)
    weight_grads[:width] += outer_sum(normed1_low, grad_query_out[...])
    weight_grads[width : 2 * width] += outer_sum(mixed[...], grad_resid[...].astype(jnp.bfloat16))
    for block in range(blocks):
        weight_grads[(2 + block) * width : (3 + block) * width] += grad_up[
            :, block * width : (block + 1) * width
        ]
    weight_grads[(2 + blocks) * width :] += outer_sum(act[...], cot)


def add_returned(wanted, returned, own, total):
    step = pl.program_id(0)
    windows = total.shape[0]
    slots = returned.shape[0]

    @pl.when(step == 0)
    def _():
        total[...] = own[...]

    for slot in range(slots):
        window = wanted[step * slots + slot]

        @pl.when(window < windows)
        def _():
            total[window] += returned[slot].astype(jnp.float32)


def value_kernel(
    wanted, returned, self_values, grad_query, tokens, weight_qkv, upstream, weight_grads, total
):
    windows, window_len, width = tokens.shape
    count = GROUP_SIZE * window_len
    add_returned(wanted, returned, self_values, total)

    @pl.when(pl.program_id(0) == pl.num_programs(0) - 1)
    def _():
        weight_grads[...] = jnp.zeros_like(weight_grads)

        @pl.loop(0, windows // GROUP_SIZE)
        def _(part):
            span = pl.ds(part * GROUP_SIZE, GROUP_SIZE)
            normed1, _ = norm_rows(tokens[span].reshape(count, width).astype(jnp.float32))
            grads = total[span].reshape(count, width).astype(jnp.bfloat16)
            queries = grad_query[span].reshape(count, width)
            partial = against(queries, weight_qkv[:, :width]) + against(
                grads, weight_qkv[:, 2 * width :]
            )
            upstream[span] = partial.reshape(GROUP_SIZE, window_len, width)
            weight_grads[...] += outer_sum(normed1.astype(jnp.bfloat16), grads)


def key_kernel(
    wanted,
    returned,
    self_keys,
    upstream,
    grad_resid,
    tokens,
    weight_qkv,
    grad_tokens,
    weight_grads,
    total,
):
    windows, window_len, width = tokens.shape
    count = GROUP_SIZE * window_len
    add_returned(wanted, returned, self_keys, total)

    @pl.when(pl.program_id(0) == pl.num_programs(0) - 1)
    def _():
        weight_grads[...] = jnp.zeros_like(weight_grads)

        @pl.loop(0, windows // GROUP_SIZE)
        def _(part):
            span = pl.ds(part * GROUP_SIZE, GROUP_SIZE)
            normed1, factor1 = norm_rows(tokens[span].reshape(count, width).astype(jnp.float32))
            grads = total[span].reshape(count, width).astype(jnp.bfloat16)
            towards = upstream[span].reshape(count, width) + against(
                grads, weight_qkv[:, width : 2 * width]
            )
            result = grad_resid[span].reshape(count, width) + norm_back(towards, normed1, factor1)
            grad_tokens[span] = result.astype(jnp.bfloat16).reshape(GROUP_SIZE, window_len, width)
            weight_grads[...] += outer_sum(normed1.astype(jnp.bfloat16), grads)


def swapped(value):
    return lax.ppermute(value, "pair", [(0, 1), (1, 0)])


def deliver(parcel):
    return lax.all_to_all(parcel, ("grp", "sp"), split_axis=0, concat_axis=0, tiled=True)


ALL = ("pair", "grp", "sp")


def sum_kernel(scatter, scale, rows, total, pair_part, pair_sum, sp_part, sp_sum, grp_part, mine, sp_full, half, pair_full, send_sems, recv_sems):
    sizes = {axis: lax.axis_size(axis) for axis in ALL}
    place = {axis: lax.axis_index(axis) for axis in ALL}
    used = [0]

    barrier = pltpu.get_barrier_semaphore()
    for axis in ALL:
        for hop in range(1, sizes[axis]):
            pl.semaphore_signal(
                barrier,
                inc=1,
                device_id={axis: lax.rem(place[axis] + hop, sizes[axis])},
                device_id_type=pl.DeviceIdType.MESH,
            )
    pl.semaphore_wait(barrier, sum(sizes[axis] - 1 for axis in ALL))

    def exchange(axis, source, landing):
        copies = []
        for hop in range(1, sizes[axis]):
            target = lax.rem(place[axis] + hop, sizes[axis])
            copy = pltpu.make_async_remote_copy(
                src_ref=source(target),
                dst_ref=landing.at[place[axis]],
                send_sem=send_sems.at[used[0]],
                recv_sem=recv_sems.at[used[0]],
                device_id={axis: target},
                device_id_type=pl.DeviceIdType.MESH,
            )
            copy.start()
            used[0] += 1
            copies.append(copy)
        landing[place[axis]] = source(place[axis])[...]
        for copy in copies:
            copy.wait()

    def added(landing):
        result = landing[0]
        for index in range(1, landing.shape[0]):
            result = result + landing[index]
        return result

    exchange("pair", lambda target: rows.at[target], pair_part)
    pieces, count, _ = pair_sum.shape
    for piece in range(pieces):
        span = slice(piece * count, (piece + 1) * count)
        pair_sum[piece] = pair_part[0, span] + pair_part[1, span]
    exchange("sp", (lambda target: pair_sum.at[target]) if scatter else (lambda _: pair_sum.at[0]), sp_part)
    sp_sum[...] = added(sp_part)
    exchange("grp", lambda _: sp_sum, grp_part)
    mine[...] = added(grp_part) * scale
    if scatter:
        exchange("sp", lambda _: mine, sp_full)
        for piece in range(pieces):
            half[piece * count : (piece + 1) * count] = sp_full[piece]
        exchange("pair", lambda _: half, pair_full)
    else:
        exchange("pair", lambda _: mine, pair_full)
    total[...] = pair_full[...]


def summed(rows, scale, collective_id):
    sp, grp = lax.axis_size("sp"), lax.axis_size("grp")
    half, width = rows.shape[0] // 2, rows.shape[1]
    scatter = half % (8 * sp) == 0
    pieces = sp if scatter else 1
    count = half // pieces
    copies = 2 + 2 * (sp - 1) + (grp - 1)

    def buffer(*shape):
        return pltpu.VMEM(shape + (width,), jnp.float32)

    total = pl.pallas_call(
        functools.partial(sum_kernel, scatter, scale),
        in_specs=[pl.BlockSpec(memory_space=pltpu.VMEM)],
        out_specs=pl.BlockSpec(memory_space=pltpu.VMEM),
        out_shape=jax.ShapeDtypeStruct((2, half, width), jnp.float32),
        scratch_shapes=[
            buffer(2, half),
            buffer(pieces, count),
            buffer(sp, count),
            buffer(count),
            buffer(grp, count),
            buffer(count),
            buffer(sp, count),
            buffer(half),
            buffer(2, half),
            pltpu.SemaphoreType.DMA((copies,)),
            pltpu.SemaphoreType.DMA((copies,)),
        ],
        compiler_params=pltpu.CompilerParams(
            collective_id=collective_id, has_side_effects=True, vmem_limit_bytes=32 * 1024 * 1024
        ),
        name="sum_gradients_%d" % collective_id,
    )(rows.reshape(2, half, width))
    return total.reshape(rows.shape)


def whole(shape):
    return pl.BlockSpec(shape, lambda *_: (0,) * len(shape))


def body(tokens, owner_ids, local_ids, weight_qkv, weight_out, weight_up, weight_down, cotangent):
    holders = lax.axis_size("grp") * lax.axis_size("sp")
    width = tokens.shape[-1]
    hidden = weight_up.shape[-1]
    windows = tokens.shape[1]
    window_len = tokens.shape[2]
    fanout = owner_ids.shape[-1]
    slots = max(2, 2 * windows * fanout // holders)
    keys_len = (fanout + 1) * window_len
    rows_total = windows * window_len
    group = GROUP_SIZE
    group_rows = group * window_len
    token_rows = tokens[0].reshape(rows_total, width)
    cot_rows = cotangent[0].reshape(rows_total, width)
    params = pltpu.CompilerParams(vmem_limit_bytes=VMEM_LIMIT)

    owners = owner_ids[0].reshape(-1)
    local_rows = local_ids[0].reshape(-1)
    onehot = (owners[:, None] == jnp.arange(holders, dtype=jnp.int32)[None, :]).astype(jnp.int32)
    ranks = jnp.sum((jnp.cumsum(onehot, axis=0) - 1) * onehot, axis=1)
    position = owners * slots + ranks
    requests = (
        jnp.full((holders * slots,), windows, jnp.int32)
        .at[position]
        .set(local_rows)
        .reshape(holders, slots)
    )
    wanted_flat = deliver(swapped(requests)).reshape(-1)

    picked = pl.pallas_call(
        pick_kernel,
        grid_spec=pltpu.PrefetchScalarGridSpec(
            num_scalar_prefetch=1,
            grid=(1,),
            in_specs=[whole((windows, window_len, width))],
            out_specs=whole((holders * slots, window_len, width)),
            scratch_shapes=[pltpu.VMEM((windows, window_len, width), jnp.bfloat16)],
        ),
        out_shape=jax.ShapeDtypeStruct((holders * slots, window_len, width), jnp.bfloat16),
        compiler_params=params,
        name="pick",
    )(wanted_flat, tokens[0])
    answered = swapped(deliver(picked.reshape(holders, slots, window_len, width)))
    answered = answered.reshape(holders * slots, window_len, width)

    blocks = hidden // width
    span_heads = HEADS * window_len
    slot_shape = (holders * slots, window_len, width)
    window_shape = (windows, window_len, width)
    grad_rows_shape = ((2 + 2 * blocks) * width, width)

    def row_spec(lanes):
        return pl.BlockSpec((group_rows, lanes), lambda i, *_: (i, 0))

    def window_spec(lanes):
        return pl.BlockSpec((group, keys_len, lanes), lambda i, *_: (i, 0, 0))

    def row_shape(lanes, kind=jnp.bfloat16):
        return jax.ShapeDtypeStruct((rows_total, lanes), kind)

    saved_specs = [
        row_spec(width),
        row_spec(width),
        row_spec(hidden),
        row_spec(hidden),
        row_spec(width),
        row_spec(width),
        row_spec(width),
        row_spec(width),
        window_spec(2 * width),
        window_spec(span_heads),
    ]
    *saved, self_values, outbound_values = pl.pallas_call(
        first_kernel,
        grid_spec=pltpu.PrefetchScalarGridSpec(
            num_scalar_prefetch=1,
            grid=(windows // group,),
            in_specs=[
                row_spec(width),
                row_spec(width),
                whole(slot_shape),
                whole((width, 3 * width)),
                whole((width, width)),
                whole((width, hidden)),
                whole((hidden, width)),
            ],
            out_specs=saved_specs + [row_spec(width), whole(slot_shape)],
        ),
        out_shape=[
            row_shape(width),
            row_shape(width),
            row_shape(hidden),
            row_shape(hidden),
            row_shape(width, jnp.float32),
            row_shape(width),
            row_shape(width),
            row_shape(width),
            jax.ShapeDtypeStruct((windows, keys_len, 2 * width), jnp.bfloat16),
            jax.ShapeDtypeStruct((windows, keys_len, span_heads), jnp.float32),
            row_shape(width, jnp.float32),
            jax.ShapeDtypeStruct(slot_shape, jnp.bfloat16),
        ],
        compiler_params=params,
        name="attend_and_tail",
    )(position, token_rows, cot_rows, answered, weight_qkv, weight_out, weight_up, weight_down)
    grad_resid = saved[4]

    def across(outbound):
        return swapped(outbound.reshape(holders, slots, window_len, width))

    outgoing_values, saved = lax.optimization_barrier((across(outbound_values), saved))
    returned_values = deliver(outgoing_values).reshape(slot_shape)

    out_rows, grad_query, self_keys, outbound_keys, tail_grads = pl.pallas_call(
        second_kernel,
        grid_spec=pltpu.PrefetchScalarGridSpec(
            num_scalar_prefetch=1,
            grid=(windows // group,),
            in_specs=[row_spec(width), row_spec(width)] + saved_specs + [whole((hidden, width))],
            out_specs=[
                row_spec(width),
                row_spec(width),
                row_spec(width),
                whole(slot_shape),
                whole(grad_rows_shape),
            ],
        ),
        out_shape=[
            row_shape(width),
            row_shape(width),
            row_shape(width, jnp.float32),
            jax.ShapeDtypeStruct(slot_shape, jnp.bfloat16),
            jax.ShapeDtypeStruct(grad_rows_shape, jnp.float32),
        ],
        compiler_params=params,
        cost_estimate=pl.CostEstimate(
            flops=40 * 10**9, bytes_accessed=150 * 10**6, transcendentals=0
        ),
        name="key_gradients",
    )(position, token_rows, cot_rows, *saved, weight_down)

    outgoing_keys, returned_values, grad_query = lax.optimization_barrier(
        (across(outbound_keys), returned_values, grad_query)
    )
    returned_keys = deliver(outgoing_keys).reshape(slot_shape)

    slot_spec = pl.BlockSpec((slots, window_len, width), lambda i, *_: (i, 0, 0))
    collect_scratch = [pltpu.VMEM(window_shape, jnp.float32)]
    upstream, value_grads = pl.pallas_call(
        value_kernel,
        grid_spec=pltpu.PrefetchScalarGridSpec(
            num_scalar_prefetch=1,
            grid=(holders,),
            in_specs=[slot_spec] + [whole(window_shape)] * 3 + [whole((width, 3 * width))],
            out_specs=[whole(window_shape), whole((width, width))],
            scratch_shapes=collect_scratch,
        ),
        out_shape=[
            jax.ShapeDtypeStruct(window_shape, jnp.float32),
            jax.ShapeDtypeStruct((width, width), jnp.float32),
        ],
        compiler_params=params,
        cost_estimate=pl.CostEstimate(
            flops=10 * 10**9, bytes_accessed=50 * 10**6, transcendentals=0
        ),
        name="collect_values",
    )(
        wanted_flat,
        returned_values,
        self_values.reshape(window_shape),
        grad_query.reshape(window_shape),
        tokens[0],
        weight_qkv,
    )
    inv_count = 1.0 / math.sqrt(2 * windows * holders * window_len)
    grad_rows, key_grads = pl.pallas_call(
        key_kernel,
        grid_spec=pltpu.PrefetchScalarGridSpec(
            num_scalar_prefetch=1,
            grid=(holders,),
            in_specs=[slot_spec] + [whole(window_shape)] * 4 + [whole((width, 3 * width))],
            out_specs=[whole(window_shape), whole((width, width))],
            scratch_shapes=collect_scratch,
        ),
        out_shape=[
            jax.ShapeDtypeStruct(window_shape, jnp.bfloat16),
            jax.ShapeDtypeStruct((width, width), jnp.float32),
        ],
        compiler_params=params,
        name="collect_keys",
    )(
        wanted_flat,
        returned_keys,
        self_keys.reshape(window_shape),
        upstream,
        grad_resid.reshape(window_shape),
        tokens[0],
        weight_qkv,
    )
    all_grads = jnp.concatenate([tail_grads, value_grads, key_grads], axis=0)
    tail_sums = summed(all_grads, inv_count, 0).reshape(4 + 2 * blocks, width, width)

    return (
        out_rows.reshape(1, windows, window_len, width),
        grad_rows[None],
        jnp.concatenate([tail_sums[0], tail_sums[3 + 2 * blocks], tail_sums[2 + 2 * blocks]], axis=1),
        tail_sums[1],
        tail_sums[2 : 2 + blocks].transpose(1, 0, 2).reshape(width, hidden),
        tail_sums[2 + blocks : 2 + 2 * blocks].reshape(hidden, width),
    )


def solution(mesh):
    in_specs = (
        P("pair", ("grp", "sp"), None, None),
        P("pair", ("grp", "sp"), None),
        P("pair", ("grp", "sp"), None),
        P(),
        P(),
        P(),
        P(),
        P("pair", ("grp", "sp"), None, None),
    )
    out_specs = (
        P("pair", ("grp", "sp"), None, None),
        P("pair", ("grp", "sp"), None, None),
        P(),
        P(),
        P(),
        P(),
    )
    return jax.shard_map(body, mesh=mesh, in_specs=in_specs, out_specs=out_specs, check_vma=False)
```
